128 devices in a mesh: row: 8 (over x, core), col: 16 (over z, y).
Axes of the slice: x: 4, y: 4, z: 4, core: 2. Of those that a mesh axis runs over, the one named last changes fastest.
Arguments:
- tokens: bfloat16 [1024, 16384], P('row', 'col'), may hold values from -6 to 6
- gate_weight: bfloat16 [16384, 26624], P('col', 'row'), may hold values from -0.046875 to 0.046875
- up_weight: bfloat16 [16384, 26624], P('col', 'row'), may hold values from -0.046875 to 0.046875
- down_weight: bfloat16 [26624, 16384], P('row', 'col'), may hold values from -0.0390625 to 0.0390625
Outputs:
- mixed: bfloat16 [1024, 16384], P('row', 'col')
The draws below stay inside these ranges and needn't reach their ends.
All inputs are finite; a program needn't handle non-finite values.
Results may differ from the reference program's by a relative error of at most 0.04.
Values may be sent and summed in bfloat16 or wider, within the bound.
No kernel may reach another device: no remote copies, remote signals or barrier semaphores. Data moves between devices by JAX's collectives and lax.ppermute only.
A program may use at most 128 MiB of HBM per device.

```python
import jax
import jax.numpy as jnp
from jax import lax

D = 16384
FFW = 26624
TOKENS = 1024
N_ROW = 8
N_COL = 16


def shard_levels(own_key, shape, shards, smallest, high):
    gain, own = 1.0, jax.random.fold_in(own_key, 6)
    for dim, blocks in shards:
        draws = jnp.exp(jax.random.uniform(jax.random.fold_in(own, dim), (blocks,), jnp.float32, smallest / len(shards), high / len(shards)))
        gain = gain * jnp.repeat(draws, shape[dim] // blocks).reshape([-1 if axis == dim else 1 for axis in range(len(shape))])
    return gain


def centred(own_key, dims, spread, limit, cuts=(), kind=jnp.bfloat16):
    array = jax.random.normal(own_key, dims, jnp.float32) * spread
    if len(cuts) > 0:
        array = shard_levels(own_key, dims, cuts, -0.22, 0.18) * array
    return jnp.clip(array, min=-limit, max=limit).astype(kind)


def setup_inputs(seed: int = 0) -> dict:
    key_of = jax.random.split(jax.random.key(seed), 5)
    tokens = centred(key_of[0], (TOKENS, D), 1.0, 6.0, ((0, 8), (1, 16)))
    gate_weight = centred(key_of[1], (D, FFW), D ** -0.5, 0.046875, ((0, 16), (1, 8)))
    up_weight = centred(key_of[2], (D, FFW), D ** -0.5, 0.046875, ((0, 16), (1, 8)))
    down_weight = centred(key_of[3], (FFW, D), FFW ** -0.5, 0.0390625, ((0, 8), (1, 16)))
    return {"tokens": tokens, "gate_weight": gate_weight, "up_weight": up_weight, "down_weight": down_weight}


def rounded(values):
    return lax.optimization_barrier(values.astype(jnp.bfloat16)).astype(jnp.float32)


def reference(tokens, gate_weight, up_weight, down_weight):
    feature_width = D // N_COL
    hidden_width = FFW // N_ROW

    def gate_block(carry, index):
        first = (index * feature_width).astype(jnp.int32)
        block = lax.dynamic_slice_in_dim(tokens, first, feature_width, 1)
        gate_rows = lax.dynamic_slice_in_dim(gate_weight, first, feature_width, 0)
        up_rows = lax.dynamic_slice_in_dim(up_weight, first, feature_width, 0)
        gate_part = rounded(jnp.dot(block, gate_rows, preferred_element_type=jnp.float32))
        up_part = rounded(jnp.dot(block, up_rows, preferred_element_type=jnp.float32))
        return (carry[0] + gate_part, carry[1] + up_part), None

    start_sums = (jnp.zeros((TOKENS, FFW), jnp.float32), jnp.zeros((TOKENS, FFW), jnp.float32))
    (gate, up), unused = lax.scan(gate_block, start_sums, jnp.arange(N_COL, dtype=jnp.int32))
    hidden = (jax.nn.silu(gate) * up).astype(jnp.bfloat16)

    def down_block(carry, index):
        first = (index * hidden_width).astype(jnp.int32)
        block = lax.dynamic_slice_in_dim(hidden, first, hidden_width, 1)
        weight_rows = lax.dynamic_slice_in_dim(down_weight, first, hidden_width, 0)
        return carry + rounded(jnp.dot(block, weight_rows, preferred_element_type=jnp.float32)), None

    mixed, unused = lax.scan(down_block, jnp.zeros((TOKENS, D), jnp.float32), jnp.arange(N_ROW, dtype=jnp.int32))
    return mixed.astype(jnp.bfloat16)
```

```python
import jax
import jax.numpy as jnp
from jax import lax
from jax.experimental import pallas as pl
from jax.experimental.pallas import tpu as pltpu
from jax.sharding import PartitionSpec as P

BF16, F32 = jnp.bfloat16, jnp.float32
RING = 4
UNIT = 16
CHUNK = 8 * UNIT
SLOT_STEPS = (0, 3, 1, 2)
LIMIT = dict(vmem_limit_bytes=48 * 1024 * 1024)
VMEM, ANY = pl.BlockSpec(memory_space=pltpu.VMEM), pl.BlockSpec(memory_space=pl.ANY)
SMEM = pl.BlockSpec(memory_space=pltpu.SMEM)


def chip_send(value, step):
    pairs = [(2 * x + c, 2 * ((x + step) % RING) + c) for x in range(RING) for c in range(2)]
    return lax.ppermute(value, "row", pairs)


def core_swap(value):
    return lax.ppermute(value, "row", [(r, r ^ 1) for r in range(2 * RING)])


def ring_send(value, axis, step):
    pairs = []
    for z in range(RING):
        for y in range(RING):
            to_z, to_y = (z, (y + step) % RING) if axis == "y" else ((z + step) % RING, y)
            pairs.append((RING * z + y, RING * to_z + to_y))
    return lax.ppermute(value, "col", pairs)


def pick_kernel(table, tokens, first, rest):
    def copy(ref, n, chain, k):
        start = chain * 64 + lax.rem(table[10 - chain] + k, RING) * UNIT
        ref[pl.ds(n * UNIT, UNIT), :] = tokens[pl.ds(pl.multiple_of(start, UNIT), UNIT), :]

    for n, (chain, k) in enumerate(((0, 2), (1, 2))):
        copy(first, n, chain, k)
    for n, (chain, k) in enumerate(((0, 1), (0, 3), (1, 1), (1, 3), (0, 0), (1, 0))):
        copy(rest, n, chain, k)


def pick(table, tokens):
    depth = tokens.shape[1]
    return pl.pallas_call(
        pick_kernel,
        in_specs=[SMEM, VMEM],
        out_specs=[VMEM] * 2,
        out_shape=[jax.ShapeDtypeStruct((n * UNIT, depth), BF16) for n in (2, 6)],
        compiler_params=pltpu.CompilerParams(**LIMIT),
    )(table, tokens)


def up_gate_kernel(first, layout, count, *refs):
    chunks = len(layout)
    sources = 4 if first is None else 1
    table, gate_w, up_w = refs[:3]
    sources = refs[3 : 3 + sources]
    outs = refs[count : count + 1 + max(place[0] for pair in layout for place in pair)]
    rows, held, stage, row_sems, in_sems, out_sems = refs[-6:]
    half = held.shape[2]
    depth = held.shape[1]
    gathers = []
    for b in range(8):
        if first is None:
            source = sources[b // 2].at[lax.rem(table[8] + b, 2)]
        else:
            source = sources[0].at[table[b], pl.ds(first, chunks)]
        gathers.append(pltpu.make_async_copy(source, rows.at[:, b], row_sems.at[b]))
    fetches = [
        pltpu.make_async_copy(
            weight.at[:, pl.ds(part * half, half)], held.at[2 * kind + part], in_sems.at[2 * kind + part]
        )
        for kind, weight in enumerate((gate_w, up_w))
        for part in range(2)
    ]
    for copy in gathers + fetches:
        copy.start()
    for copy in gathers:
        copy.wait()
    leaves = []
    for n in range(4):
        kind, part = n // 2, n % 2
        fetches[n].wait()
        value = jnp.dot(
            rows[...].reshape(chunks * CHUNK, depth), held[n], preferred_element_type=F32
        ).astype(BF16)
        for c in range(chunks):
            stage[c, kind, :, pl.ds(part * half, half)] = value[c * CHUNK : (c + 1) * CHUNK]
            out, block = layout[c][kind]
            leave = pltpu.make_async_copy(
                stage.at[c, kind, :, pl.ds(part * half, half)],
                outs[out].at[pl.ds(block * CHUNK, CHUNK), pl.ds(part * half, half)],
                out_sems.at[n * chunks + c],
            )
            leave.start()
            leaves.append(leave)
    for leave in leaves:
        leave.wait()


def up_gate(sources, first, layout, table, gate_w, up_w, after=()):
    depth, width = gate_w.shape
    chunks = len(layout)
    places = [place for pair in layout for place in pair]
    outs = 1 + max(place[0] for place in places)
    shape = (CHUNK * (1 + max(place[1] for place in places)), width)
    operands = [table, gate_w, up_w, *sources, *after]
    return pl.pallas_call(
        lambda *refs: up_gate_kernel(first, layout, len(operands), *refs),
        in_specs=[SMEM] + [ANY] * (len(operands) - 1),
        out_specs=[ANY] * outs,
        out_shape=[jax.ShapeDtypeStruct(shape, BF16)] * outs,
        scratch_shapes=[
            pltpu.VMEM((chunks, 8, UNIT, depth), BF16),
            pltpu.VMEM((4, depth, width // 2), BF16),
            pltpu.VMEM((chunks, 2, CHUNK, width), BF16),
            pltpu.SemaphoreType.DMA((8,)),
            pltpu.SemaphoreType.DMA((4,)),
            pltpu.SemaphoreType.DMA((4 * chunks,)),
        ],
        compiler_params=pltpu.CompilerParams(**LIMIT),
        cost_estimate=pl.CostEstimate(
            flops=4 * chunks * CHUNK * depth * width,
            bytes_accessed=4 * depth * width + chunks * CHUNK * (depth + 2 * width) * 2,
            transcendentals=0,
        ),
    )(*operands)


def down_kernel(slots, count, *refs):
    table, weight = refs[:2]
    per_slot = 2 if refs[2].shape[0] == CHUNK else 4
    pieces = refs[2 : 2 + per_slot * len(slots)]
    mine, other, rows, held, stage, row_sems, sems, out_sems = refs[count:]
    core = table[8]
    height = CHUNK * 2 // per_slot
    gathers = [
        pltpu.make_async_copy(source, rows.at[pl.ds(n * height, height)], row_sems.at[n])
        for n, source in enumerate(pieces)
    ]
    depth = held.shape[0]
    cut = depth // 512 * 256 + 256
    cuts = ((0, cut), (cut, depth - cut))
    fetches = [
        pltpu.make_async_copy(weight.at[pl.ds(start, size)], held.at[pl.ds(start, size)], sems.at[n])
        for n, (start, size) in enumerate(cuts)
    ]
    for copy in gathers + fetches:
        copy.start()
    for copy in gathers:
        copy.wait()
    total = None
    for fetch, (start, size) in zip(fetches, cuts):
        fetch.wait()
        part = jnp.dot(
            rows[:, start : start + size], held[start : start + size], preferred_element_type=F32
        )
        total = part if total is None else total + part
    total = total.astype(BF16).reshape(len(slots), 2, 2, RING, UNIT, total.shape[1])
    for s in range(len(slots)):
        for chain in range(2):
            for c in range(2):
                for dx in range(RING):
                    stage[c, s, dx, chain] = total[s, chain, c, dx]
    leaves = []
    for s, slot in enumerate(slots):
        leaves.append(pltpu.make_async_copy(stage.at[core, s], mine.at[:, slot], out_sems.at[2 * s]))
        leaves.append(pltpu.make_async_copy(stage.at[1 - core, s], other.at[:, slot], out_sems.at[2 * s + 1]))
    for leave in leaves:
        leave.start()
    for leave in leaves:
        leave.wait()


def down(table, slots, pieces, weight, held_outs, after=()):
    depth, width = weight.shape
    tokens = 2 * CHUNK * len(slots)
    shape = (RING, 4, 2, UNIT, width)
    operands = [table, weight, *pieces, *after]
    aliases = {}
    if held_outs is not None:
        aliases = {len(operands): 0, len(operands) + 1: 1}
        operands += held_outs
    return pl.pallas_call(
        lambda *refs: down_kernel(slots, len(operands), *refs),
        in_specs=[SMEM] + [ANY] * (len(operands) - 1),
        out_specs=[ANY] * 2,
        out_shape=[jax.ShapeDtypeStruct(shape, BF16)] * 2,
        input_output_aliases=aliases,
        scratch_shapes=[
            pltpu.VMEM((tokens, depth), BF16),
            pltpu.VMEM((depth, width), BF16),
            pltpu.VMEM((2, len(slots), RING, 2, UNIT, width), BF16),
            pltpu.SemaphoreType.DMA((len(pieces),)),
            pltpu.SemaphoreType.DMA((2,)),
            pltpu.SemaphoreType.DMA((2 * len(slots),)),
        ],
        compiler_params=pltpu.CompilerParams(**LIMIT),
        cost_estimate=pl.CostEstimate(
            flops=2 * tokens * depth * width,
            bytes_accessed=2 * (depth * width + tokens * (depth + width)),
            transcendentals=0,
        ),
    )(*operands)


def place_kernel(table, *refs):
    pieces, outs = refs[:8], refs[8:]
    for chain in range(2):
        for k in range(RING):
            start = lax.rem(table[9 + chain] + k, RING) * UNIT
            for core in range(2):
                outs[chain][pl.ds(pl.multiple_of(start + core * 64, UNIT), UNIT), :] = pieces[4 * chain + k][
                    pl.ds(core * UNIT, UNIT), :
                ]


def place(table, pieces):
    width = pieces[0].shape[1]
    return pl.pallas_call(
        place_kernel,
        in_specs=[SMEM] + [VMEM] * 8,
        out_specs=[VMEM] * 2,
        out_shape=[jax.ShapeDtypeStruct((CHUNK, width), BF16)] * 2,
        compiler_params=pltpu.CompilerParams(**LIMIT),
    )(table, *pieces)


def half_kernel(core, value, *refs):
    out, sem = refs[-2:]
    copy = pltpu.make_async_copy(value.at[pl.ds(core * 64, 64)], out, sem)
    copy.start()
    copy.wait()


def half(value, core, after):
    return pl.pallas_call(
        lambda *refs: half_kernel(core, *refs),
        in_specs=[ANY] * (1 + len(after)),
        out_specs=ANY,
        out_shape=jax.ShapeDtypeStruct((64, value.shape[1]), BF16),
        scratch_shapes=[pltpu.SemaphoreType.DMA],
        compiler_params=pltpu.CompilerParams(**LIMIT),
    )(value, *after)


def share_kernel(mine, theirs, own, one, two, three):
    for dx, out in enumerate((own, one, two, three)):
        total = mine[dx].astype(F32) + theirs[dx].astype(F32)
        out[...] = total.reshape(out.shape).astype(out.dtype)


def share(mine, theirs):
    width = mine.shape[-1]
    return pl.pallas_call(
        share_kernel,
        in_specs=[VMEM] * 2,
        out_specs=[VMEM] * 4,
        out_shape=[jax.ShapeDtypeStruct((CHUNK, width), kind) for kind in (F32, BF16, BF16, BF16)],
        compiler_params=pltpu.CompilerParams(**LIMIT),
    )(mine, theirs)


def finish_kernel(table, own, one, two, three, out):
    total = own[...] + one[...].astype(F32) + two[...].astype(F32) + three[...].astype(F32)
    total = total.astype(BF16)
    for n, k in enumerate(SLOT_STEPS):
        for chain in range(2):
            start = chain * 64 + lax.rem(table[10 - chain] + k, RING) * UNIT
            out[pl.ds(pl.multiple_of(start, UNIT), UNIT), :] = total[
                (2 * n + chain) * UNIT : (2 * n + chain + 1) * UNIT
            ]


def finish(table, terms):
    return pl.pallas_call(
        finish_kernel,
        in_specs=[SMEM] + [VMEM] * 4,
        out_specs=VMEM,
        out_shape=jax.ShapeDtypeStruct((CHUNK, terms[0].shape[1]), BF16),
        compiler_params=pltpu.CompilerParams(**LIMIT),
    )(table, *terms)


def added(*values):
    total = values[0].astype(F32)
    for value in values[1:]:
        total = total + value.astype(F32)
    return total


def body(tokens, gate_w, up_w, down_w):
    col, row = lax.axis_index("col"), lax.axis_index("row")
    z, y, x, core = col // RING, col % RING, row // 2, row % 2
    table = [2 * ((x - b // 2) % RING) + b % 2 for b in range(8)] + [core, z, y]
    table = jnp.stack(table).astype(jnp.int32)

    mine, rest = pick(table, tokens)
    pair = jnp.concatenate([mine, core_swap(mine)], axis=0).reshape(2, 2, UNIT, -1)
    quarters = [pair, chip_send(pair, 1), chip_send(pair, 2), chip_send(pair, -1)]
    rest = lax.all_gather(rest, "row", axis=0, tiled=False).reshape(8, 6, UNIT, -1)

    far = up_gate(quarters, None, [[(0, 0), (1, 0)], [(2, 0), (3, 0)]], table, gate_w, up_w)
    routes = [("y", 1), ("y", -1), ("z", 1), ("z", -1)]
    first = [ring_send(value, *route) for value, route in zip(far, routes)]
    beside = up_gate(
        [rest], 0, [[(0, 0), (0, 1)], [(1, 1), (1, 0)], [(2, 0), (2, 1)], [(3, 1), (3, 0)]], table, gate_w, up_w
    )
    passed = [
        both.at[:CHUNK].set(added(both[:CHUNK], value).astype(BF16)) for both, value in zip(beside, first)
    ]
    second = [ring_send(value, *route) for value, route in zip(passed, routes)]
    near = up_gate([rest], 4, [[(0, 0), (1, 0)], [(2, 0), (3, 0)]], table, gate_w, up_w, after=passed)

    hidden = []
    block = 2 * UNIT
    for chain, (axis, at) in enumerate((("z", z), ("y", y))):
        forward, backward = second[2 * chain : 2 * chain + 2]
        terms = [
            ((near[2 * chain], 0), (forward, 0), (backward, CHUNK)),
            ((near[2 * chain + 1], 0), (backward, 0), (forward, CHUNK)),
        ]

        def part(k, kind):
            start = (at + k) % RING * block
            return added(
                *[lax.dynamic_slice_in_dim(term, base + start, block, 0) for term, base in terms[kind]]
            )

        ahead = jnp.concatenate([part(2, 0), part(1, 1)], axis=0).astype(BF16)
        behind = jnp.concatenate([part(2, 1), part(3, 0)], axis=0).astype(BF16)
        ahead, behind = ring_send(ahead, axis, 1), ring_send(behind, axis, -1)
        more = ring_send(added(part(1, 0), ahead[:block]).astype(BF16), axis, 1)
        less = ring_send(added(part(3, 1), behind[:block]).astype(BF16), axis, -1)
        gate = added(part(0, 0), behind[block:], more)
        up = added(part(0, 1), ahead[block:], less)
        hidden.append((jax.nn.silu(gate) * up).astype(BF16))

    pieces = []
    for value, axis in zip(hidden, ("z", "y")):
        pieces += [value, ring_send(value, axis, -1), ring_send(value, axis, 2), ring_send(value, axis, 1)]
    own = place(table, pieces)

    behind = [ring_send(value, axis, 1) for value, axis in zip(own, "yz")]
    ahead = [ring_send(value, axis, -1) for value, axis in zip(own, "yz")]
    sums = down(table, (0,), own, down_w, None)
    onward = [(half(b, 0, sums), half(a, 1, sums)) for b, a in zip(behind, ahead)]
    distant = []
    for (forward, backward), axis in zip(onward, "yz"):
        distant += [ring_send(forward, axis, 1), ring_send(backward, axis, -1)]
    sums = down(table, (1, 2), [*behind, *ahead], down_w, sums, after=[*onward[0], *onward[1]])
    mine, other = down(table, (3,), distant, down_w, sums)

    total, *sent = share(mine, core_swap(other))
    return finish(table, [total] + [chip_send(value, step) for value, step in zip(sent, (-1, 2, 1))])


def solution(mesh):
    placed = (P("row", "col"), P("col", "row"), P("col", "row"), P("row", "col"))
    return jax.shard_map(
        body, mesh=mesh, in_specs=placed, out_specs=P("row", "col"), check_vma=False
    )
```

```python
import jax
import jax.numpy as jnp
from jax import lax
from jax.experimental import pallas as pl
from jax.experimental.pallas import tpu as pltpu
from jax.sharding import PartitionSpec as P

BF16, F32 = jnp.bfloat16, jnp.float32
RING = 4
UNIT = 16
CHUNK = 8 * UNIT
SLOT_STEPS = ((0, 3, 1), (2,))
LIMIT = dict(vmem_limit_bytes=14 * 1024 * 1024)
VMEM, ANY = pl.BlockSpec(memory_space=pltpu.VMEM), pl.BlockSpec(memory_space=pl.ANY)
SMEM = pl.BlockSpec(memory_space=pltpu.SMEM)


def chip_send(value, step):
    pairs = [(2 * x + c, 2 * ((x + step) % RING) + c) for x in range(RING) for c in range(2)]
    return lax.ppermute(value, "row", pairs)


def core_swap(value):
    return lax.ppermute(value, "row", [(r, r ^ 1) for r in range(2 * RING)])


def ring_send(value, axis, step):
    pairs = []
    for z in range(RING):
        for y in range(RING):
            to_z, to_y = (z, (y + step) % RING) if axis == "y" else ((z + step) % RING, y)
            pairs.append((RING * z + y, RING * to_z + to_y))
    return lax.ppermute(value, "col", pairs)


def preload(weights, after):
    count, parts = len(weights), 4

    def kernel(*refs):
        sources, outs, sems = refs[:count], refs[-1 - count : -1], refs[-1]
        copies = []
        for m in range(count):
            rows = sources[m].shape[0] // parts
            for n in range(parts):
                block = pl.ds(n * rows, rows)
                copies.append(
                    pltpu.make_async_copy(sources[m].at[block], outs[m].at[block], sems.at[m * parts + n])
                )
        for copy in copies:
            copy.start()
        for copy in copies:
            copy.wait()

    return pl.pallas_call(
        kernel,
        in_specs=[ANY] * (count + len(after)),
        out_specs=[VMEM] * count,
        out_shape=[jax.ShapeDtypeStruct(weight.shape, BF16) for weight in weights],
        scratch_shapes=[pltpu.SemaphoreType.DMA((count * parts,))],
        compiler_params=pltpu.CompilerParams(vmem_limit_bytes=38 * 1024 * 1024),
        cost_estimate=pl.CostEstimate(
            flops=0, bytes_accessed=4 * sum(weight.size for weight in weights), transcendentals=0
        ),
    )(*weights, *after)


def tile_cuts(size):
    step = size // 1024 * 256
    return [(n * step, step) for n in range(3)] + [(3 * step, size - 3 * step)]


def pick_kernel(table, tokens, first, rest):
    def copy(ref, n, chain, k):
        start = chain * 64 + lax.rem(table[10 - chain] + k, RING) * UNIT
        ref[pl.ds(n * UNIT, UNIT), :] = tokens[pl.ds(pl.multiple_of(start, UNIT), UNIT), :]

    for n, (chain, k) in enumerate(((0, 2), (1, 2))):
        copy(first, n, chain, k)
    for n, (chain, k) in enumerate(((0, 1), (0, 3), (1, 1), (1, 3), (0, 0), (1, 0))):
        copy(rest, n, chain, k)


def pick(table, tokens):
    depth = tokens.shape[1]
    return pl.pallas_call(
        pick_kernel,
        in_specs=[SMEM, VMEM],
        out_specs=[VMEM] * 2,
        out_shape=[jax.ShapeDtypeStruct((n * UNIT, depth), BF16) for n in (2, 6)],
        compiler_params=pltpu.CompilerParams(**LIMIT),
    )(table, tokens)


def up_gate_kernel(first, layout, count, *refs):
    chunks = len(layout)
    table, gate_w, up_w = refs[:3]
    quarters = refs[3:7]
    outs, rows = refs[count:-1], refs[-1]
    width = gate_w.shape[1]
    for b in range(8):
        core = lax.rem(table[8] + b, 2)
        for c in range(chunks):
            rows[pl.ds(c * CHUNK + b * UNIT, UNIT), :] = quarters[b // 2][core, first + c]
    for kind, weight in enumerate((gate_w, up_w)):
        for start, size in tile_cuts(width):
            value = jnp.dot(
                rows[...], weight[:, start : start + size], preferred_element_type=F32
            ).astype(BF16)
            for c in range(chunks):
                out, block = layout[c][kind]
                outs[out][pl.ds(block * CHUNK, CHUNK), pl.ds(start, size)] = value[
                    c * CHUNK : (c + 1) * CHUNK
                ]


def up_gate(quarters, first, layout, table, gate_w, up_w, after=()):
    depth, width = gate_w.shape
    chunks = len(layout)
    places = [place for pair in layout for place in pair]
    outs = 1 + max(place[0] for place in places)
    shape = (CHUNK * (1 + max(place[1] for place in places)), width)
    operands = [table, gate_w, up_w, *quarters, *after]
    return pl.pallas_call(
        lambda *refs: up_gate_kernel(first, layout, len(operands), *refs),
        in_specs=[SMEM] + [VMEM] * 6 + [ANY] * len(after),
        out_specs=[VMEM] * outs,
        out_shape=[jax.ShapeDtypeStruct(shape, BF16)] * outs,
        scratch_shapes=[pltpu.VMEM((chunks * CHUNK, depth), BF16)],
        compiler_params=pltpu.CompilerParams(**LIMIT),
        cost_estimate=pl.CostEstimate(
            flops=4 * chunks * CHUNK * depth * width,
            bytes_accessed=4 * depth * width + chunks * CHUNK * (depth + 2 * width) * 2,
            transcendentals=0,
        ),
    )(*operands)


def down_kernel(count, slots, *refs):
    table, weight = refs[:2]
    pieces = refs[2 : 2 + count]
    mine, other, rows, stage = refs[-4:]
    core = table[8]
    height = rows.shape[0] // count
    for n, piece in enumerate(pieces):
        rows[pl.ds(n * height, height), :] = piece[...]
    for start, size in tile_cuts(weight.shape[1]):
        part = jnp.dot(rows[...], weight[:, start : start + size], preferred_element_type=F32)
        part = part.astype(BF16).reshape(slots, 2, 2, RING, UNIT, size)
        for s in range(slots):
            for chain in range(2):
                for c in range(2):
                    for dx in range(RING):
                        stage[c, dx, s, chain, :, pl.ds(start, size)] = part[s, chain, c, dx]
    mine[...] = stage[core]
    other[...] = stage[1 - core]


def down(table, slots, pieces, weight, after=()):
    depth, width = weight.shape
    tokens = 2 * CHUNK * slots
    shape = (RING, slots, 2, UNIT, width)
    operands = [table, weight, *pieces, *after]
    return pl.pallas_call(
        lambda *refs: down_kernel(len(pieces), slots, *refs),
        in_specs=[SMEM] + [VMEM] * (1 + len(pieces)) + [ANY] * len(after),
        out_specs=[VMEM] * 2,
        out_shape=[jax.ShapeDtypeStruct(shape, BF16)] * 2,
        scratch_shapes=[pltpu.VMEM((tokens, depth), BF16), pltpu.VMEM((2,) + shape, BF16)],
        compiler_params=pltpu.CompilerParams(**LIMIT),
        cost_estimate=pl.CostEstimate(
            flops=2 * tokens * depth * width,
            bytes_accessed=2 * (depth * width + tokens * (depth + width)),
            transcendentals=0,
        ),
    )(*operands)


def place_kernel(table, *refs):
    pieces, outs = refs[:8], refs[8:]
    for chain in range(2):
        for k in range(RING):
            start = lax.rem(table[9 + chain] + k, RING) * UNIT
            for core in range(2):
                outs[chain][pl.ds(pl.multiple_of(start + core * 64, UNIT), UNIT), :] = pieces[4 * chain + k][
                    pl.ds(core * UNIT, UNIT), :
                ]


def place(table, pieces):
    width = pieces[0].shape[1]
    return pl.pallas_call(
        place_kernel,
        in_specs=[SMEM] + [VMEM] * 8,
        out_specs=[VMEM] * 2,
        out_shape=[jax.ShapeDtypeStruct((CHUNK, width), BF16)] * 2,
        compiler_params=pltpu.CompilerParams(**LIMIT),
    )(table, *pieces)


def half(value, core, after):
    def kernel(value, *refs):
        refs[-1][...] = value[pl.ds(core * 64, 64), :]

    return pl.pallas_call(
        kernel,
        in_specs=[VMEM] + [ANY] * len(after),
        out_specs=VMEM,
        out_shape=jax.ShapeDtypeStruct((64, value.shape[1]), BF16),
        compiler_params=pltpu.CompilerParams(**LIMIT),
    )(value, *after)


def behind_of(value, after):
    return pl.pallas_call(
        lambda *refs: None,
        in_specs=[ANY] * (1 + len(after)),
        out_specs=ANY,
        out_shape=jax.ShapeDtypeStruct(value.shape, value.dtype),
        input_output_aliases={0: 0},
        compiler_params=pltpu.CompilerParams(**LIMIT),
    )(value, *after)


def share_kernel(count, *refs):
    pairs, outs = refs[: 2 * count], refs[2 * count :]
    first = 0
    for mine, theirs in zip(pairs[:count], pairs[count:]):
        rows = mine.shape[1] * 2 * UNIT
        for dx, out in enumerate(outs):
            total = mine[dx].astype(F32) + theirs[dx].astype(F32)
            out[pl.ds(first, rows), :] = total.reshape(rows, out.shape[1]).astype(out.dtype)
        first += rows


def share(mine, theirs):
    rows, width = sum(value.shape[1] for value in mine) * 2 * UNIT, mine[0].shape[-1]
    return pl.pallas_call(
        lambda *refs: share_kernel(len(mine), *refs),
        in_specs=[VMEM] * (2 * len(mine)),
        out_specs=[VMEM] * 4,
        out_shape=[jax.ShapeDtypeStruct((rows, width), kind) for kind in (F32, BF16, BF16, BF16)],
        compiler_params=pltpu.CompilerParams(**LIMIT),
    )(*mine, *theirs)


def finish_kernel(table, *refs):
    terms, out = refs[:8], refs[8]
    for batch, steps in enumerate(SLOT_STEPS):
        own, *sent = terms[4 * batch : 4 * batch + 4]
        total = own[...]
        for block in sent:
            total = total + block[...].astype(F32)
        total = total.astype(BF16)
        for n, k in enumerate(steps):
            for chain in range(2):
                start = chain * 64 + lax.rem(table[10 - chain] + k, RING) * UNIT
                out[pl.ds(pl.multiple_of(start, UNIT), UNIT), :] = total[
                    (2 * n + chain) * UNIT : (2 * n + chain + 1) * UNIT
                ]


def finish(table, terms):
    return pl.pallas_call(
        finish_kernel,
        in_specs=[SMEM] + [VMEM] * 8,
        out_specs=VMEM,
        out_shape=jax.ShapeDtypeStruct((CHUNK, terms[0].shape[1]), BF16),
        compiler_params=pltpu.CompilerParams(**LIMIT),
    )(table, *terms)


def pass_on(both, received):
    def kernel(both, received, out):
        out[:CHUNK, :] = (both[:CHUNK, :].astype(F32) + received[...].astype(F32)).astype(BF16)

    return pl.pallas_call(
        kernel,
        in_specs=[VMEM] * 2,
        out_specs=VMEM,
        out_shape=jax.ShapeDtypeStruct(both.shape, BF16),
        input_output_aliases={0: 0},
        compiler_params=pltpu.CompilerParams(**LIMIT),
    )(both, received)


def blend_kernel(at, outs_parts, act, count, *refs):
    table, arrays, outs = refs[0], refs[1:count], refs[count:]
    height = 2 * UNIT

    def total_of(part):
        total = None
        for array, base, k in part:
            start = base
            if k is not None:
                start = pl.multiple_of(base + lax.rem(table[at] + k, RING) * height, height)
            value = arrays[array][pl.ds(start, height), :].astype(F32)
            total = value if total is None else total + value
        return total

    for parts, out in zip(outs_parts, outs):
        if act:
            gate, up = (total_of(part) for part in parts)
            out[...] = (gate / (1.0 + jnp.exp(-gate)) * up).astype(BF16)
        else:
            for m, part in enumerate(parts):
                out[pl.ds(m * height, height), :] = total_of(part).astype(BF16)


def blend(table, at, arrays, outs_parts, act=False):
    width = arrays[0].shape[1]
    count = 1 + len(arrays)
    heights = [2 * UNIT * (1 if act else len(parts)) for parts in outs_parts]
    return pl.pallas_call(
        lambda *refs: blend_kernel(at, outs_parts, act, count, *refs),
        in_specs=[SMEM] + [VMEM] * len(arrays),
        out_specs=[VMEM] * len(outs_parts),
        out_shape=[jax.ShapeDtypeStruct((height, width), BF16) for height in heights],
        compiler_params=pltpu.CompilerParams(**LIMIT),
    )(table, *arrays)


def body(tokens, gate_w, up_w, down_w):
    col, row = lax.axis_index("col"), lax.axis_index("row")
    z, y, x, core = col // RING, col % RING, row // 2, row % 2
    table = [2 * ((x - b // 2) % RING) + b % 2 for b in range(8)] + [core, z, y]
    table = jnp.stack(table).astype(jnp.int32)

    quarters = []
    for mine in pick(table, tokens):
        pair = jnp.stack([mine, core_swap(mine)]).reshape(2, mine.shape[0] // UNIT, UNIT, -1)
        quarters.append([pair, chip_send(pair, 1), chip_send(pair, 2), chip_send(pair, -1)])
    quarters, rest = quarters

    gate_w, up_w = preload((gate_w, up_w), after=quarters[:1])

    far = up_gate(quarters, 0, [[(0, 0), (1, 0)], [(2, 0), (3, 0)]], table, gate_w, up_w)
    routes = [("y", 1), ("y", -1), ("z", 1), ("z", -1)]
    first = [ring_send(value, *route) for value, route in zip(far, routes)]
    beside = up_gate(
        rest, 0, [[(0, 0), (0, 1)], [(1, 1), (1, 0)], [(2, 0), (2, 1)], [(3, 1), (3, 0)]], table, gate_w, up_w
    )
    passed = [pass_on(both, value) for both, value in zip(beside, first)]
    second = [ring_send(value, *route) for value, route in zip(passed, routes)]
    near = up_gate(rest, 4, [[(0, 0), (1, 0)], [(2, 0), (3, 0)]], table, gate_w, up_w, after=passed)

    hidden = []
    gate = lambda k: [(0, 0, k), (2, 0, k), (3, CHUNK, k)]
    up = lambda k: [(1, 0, k), (3, 0, k), (2, CHUNK, k)]
    for chain, (axis, at) in enumerate((("z", 9), ("y", 10))):
        arrays = [*near[2 * chain : 2 * chain + 2], *second[2 * chain : 2 * chain + 2]]
        ahead, behind = blend(table, at, arrays, [[gate(2), up(1)], [up(2), gate(3)]])
        arrays += [ring_send(ahead, axis, 1), ring_send(behind, axis, -1)]
        more, less = blend(
            table, at, arrays, [[gate(1) + [(4, 0, None)]], [up(3) + [(5, 0, None)]]]
        )
        arrays += [ring_send(more, axis, 1), ring_send(less, axis, -1)]
        block = 2 * UNIT
        terms = [gate(0) + [(5, block, None), (6, 0, None)], up(0) + [(4, block, None), (7, 0, None)]]
        hidden += blend(table, at, arrays, [terms], act=True)

    pieces = []
    for value, axis in zip(hidden, ("z", "y")):
        pieces += [value, ring_send(value, axis, -1), ring_send(value, axis, 2), ring_send(value, axis, 1)]
    own = place(table, pieces)

    behind = [ring_send(value, axis, 1) for value, axis in zip(own, "yz")]
    ahead = [ring_send(value, axis, -1) for value, axis in zip(own, "yz")]
    sums = down(table, 1, own, down_w)
    onward = [(half(b, 0, sums), half(a, 1, sums)) for b, a in zip(behind, ahead)]
    distant = []
    for (forward, backward), axis in zip(onward, "yz"):
        distant += [ring_send(forward, axis, 1), ring_send(backward, axis, -1)]
    more = down(table, 2, [*behind, *ahead], down_w, after=[*onward[0], *onward[1]])
    last = down(table, 1, distant, down_w)

    terms = []
    batches = [[sums, (more[0], behind_of(more[1], distant))], [last]]
    for batch in batches:
        own_total, *sent = share([mine for mine, other in batch], [core_swap(other) for mine, other in batch])
        terms += [own_total] + [chip_send(value, step) for value, step in zip(sent, (-1, 2, 1))]
    return finish(table, terms)


def solution(mesh):
    placed = (P("row", "col"), P("col", "row"), P("col", "row"), P("row", "col"))
    return jax.shard_map(
        body, mesh=mesh, in_specs=placed, out_specs=P("row", "col"), check_vma=False
    )
```

```python
import jax
import jax.numpy as jnp
from jax import lax
from jax.experimental import pallas as pl
from jax.experimental.pallas import tpu as pltpu
from jax.sharding import PartitionSpec as P

BF16, F32 = jnp.bfloat16, jnp.float32
RING = 4
UNIT = 16
CHUNK = 8 * UNIT
SLOT_STEPS = ((0, 3, 1), (2,))
LIMIT = dict(vmem_limit_bytes=14 * 1024 * 1024)
VMEM, ANY = pl.BlockSpec(memory_space=pltpu.VMEM), pl.BlockSpec(memory_space=pl.ANY)
SMEM = pl.BlockSpec(memory_space=pltpu.SMEM)


def chip_send(value, step):
    pairs = [(2 * x + c, 2 * ((x + step) % RING) + c) for x in range(RING) for c in range(2)]
    return lax.ppermute(value, "row", pairs)


def core_swap(value):
    return lax.ppermute(value, "row", [(r, r ^ 1) for r in range(2 * RING)])


def ring_send(value, axis, step):
    pairs = []
    for z in range(RING):
        for y in range(RING):
            to_z, to_y = (z, (y + step) % RING) if axis == "y" else ((z + step) % RING, y)
            pairs.append((RING * z + y, RING * to_z + to_y))
    return lax.ppermute(value, "col", pairs)


def tile_cuts(size):
    step = size // 1024 * 256
    return [(n * step, step) for n in range(3)] + [(3 * step, size - 3 * step)]


def pick_kernel(table, tokens, first, rest):
    def copy(ref, n, chain, k):
        start = chain * 64 + lax.rem(table[10 - chain] + k, RING) * UNIT
        ref[pl.ds(n * UNIT, UNIT), :] = tokens[pl.ds(pl.multiple_of(start, UNIT), UNIT), :]

    for n, (chain, k) in enumerate(((0, 2), (1, 2))):
        copy(first, n, chain, k)
    for n, (chain, k) in enumerate(((0, 1), (0, 3), (1, 1), (1, 3), (0, 0), (1, 0))):
        copy(rest, n, chain, k)


def pick(table, tokens):
    depth = tokens.shape[1]
    return pl.pallas_call(
        pick_kernel,
        in_specs=[SMEM, VMEM],
        out_specs=[VMEM] * 2,
        out_shape=[jax.ShapeDtypeStruct((n * UNIT, depth), BF16) for n in (2, 6)],
        compiler_params=pltpu.CompilerParams(**LIMIT),
        cost_estimate=pl.CostEstimate(flops=2 * 10**10, bytes_accessed=0, transcendentals=0),
    )(table, tokens)


def up_gate_kernel(first, layout, count, *refs):
    chunks = len(layout)
    table, gate_w, up_w = refs[:3]
    halves = refs[3:5]
    outs, rows = refs[count:-1], refs[-1]
    width = gate_w.shape[1]
    for n, half in enumerate(halves):
        core = table[8] if n == 0 else 1 - table[8]
        for dx in range(RING):
            for c in range(chunks):
                start = pl.multiple_of(c * CHUNK + 2 * dx * UNIT + core * UNIT, UNIT)
                rows[pl.ds(start, UNIT), :] = half[dx, first + c]
    for kind, weight in enumerate((gate_w, up_w)):
        for start, size in tile_cuts(width):
            value = jnp.dot(
                rows[...], weight[:, start : start + size], preferred_element_type=F32
            ).astype(BF16)
            for c in range(chunks):
                out, block = layout[c][kind]
                outs[out][pl.ds(block * CHUNK, CHUNK), pl.ds(start, size)] = value[
                    c * CHUNK : (c + 1) * CHUNK
                ]


def up_gate(halves, first, layout, table, gate_w, up_w, after=()):
    depth, width = gate_w.shape
    chunks = len(layout)
    places = [place for pair in layout for place in pair]
    outs = 1 + max(place[0] for place in places)
    shape = (CHUNK * (1 + max(place[1] for place in places)), width)
    operands = [table, gate_w, up_w, *halves, *after]
    return pl.pallas_call(
        lambda *refs: up_gate_kernel(first, layout, len(operands), *refs),
        in_specs=[SMEM] + [VMEM] * 4 + [ANY] * len(after),
        out_specs=[VMEM] * outs,
        out_shape=[jax.ShapeDtypeStruct(shape, BF16)] * outs,
        scratch_shapes=[pltpu.VMEM((chunks * CHUNK, depth), BF16)],
        compiler_params=pltpu.CompilerParams(**LIMIT),
        cost_estimate=pl.CostEstimate(
            flops=4 * chunks * CHUNK * depth * width,
            bytes_accessed=4 * depth * width + chunks * CHUNK * (depth + 2 * width) * 2,
            transcendentals=0,
        ),
    )(*operands)


def down_kernel(count, slots, *refs):
    table, weight = refs[:2]
    pieces = refs[2 : 2 + count]
    outs, (rows, stage) = refs[-2 - 2 * slots : -2], refs[-2:]
    core = table[8]
    height = rows.shape[0] // count
    for n, piece in enumerate(pieces):
        rows[pl.ds(n * height, height), :] = piece[...]
    for start, size in tile_cuts(weight.shape[1]):
        part = jnp.dot(rows[...], weight[:, start : start + size], preferred_element_type=F32)
        part = part.astype(BF16).reshape(slots, 2, 2, RING, UNIT, size)
        for s in range(slots):
            for chain in range(2):
                for c in range(2):
                    for dx in range(RING):
                        stage[c, s, dx, chain, :, pl.ds(start, size)] = part[s, chain, c, dx]
    for s in range(slots):
        outs[2 * s][...] = stage[core, s]
        outs[2 * s + 1][...] = stage[1 - core, s]


def down(table, slots, pieces, weight, after=()):
    depth, width = weight.shape
    tokens = 2 * CHUNK * slots
    shape = (RING, 2, UNIT, width)
    operands = [table, weight, *pieces, *after]
    outs = pl.pallas_call(
        lambda *refs: down_kernel(len(pieces), slots, *refs),
        in_specs=[SMEM] + [VMEM] * (1 + len(pieces)) + [ANY] * len(after),
        out_specs=[VMEM] * (2 * slots),
        out_shape=[jax.ShapeDtypeStruct(shape, BF16)] * (2 * slots),
        scratch_shapes=[pltpu.VMEM((tokens, depth), BF16), pltpu.VMEM((2, slots) + shape, BF16)],
        compiler_params=pltpu.CompilerParams(**LIMIT),
        cost_estimate=pl.CostEstimate(
            flops=2 * tokens * depth * width,
            bytes_accessed=2 * (depth * width + tokens * (depth + width)),
            transcendentals=0,
        ),
    )(*operands)
    return [(outs[2 * s], outs[2 * s + 1]) for s in range(slots)]


def place_kernel(table, *refs):
    pieces, outs = refs[:8], refs[8:]
    for chain in range(2):
        for k in range(RING):
            start = lax.rem(table[9 + chain] + k, RING) * UNIT
            for core in range(2):
                outs[chain][pl.ds(pl.multiple_of(start + core * 64, UNIT), UNIT), :] = pieces[4 * chain + k][
                    pl.ds(core * UNIT, UNIT), :
                ]


def place(table, pieces):
    width = pieces[0].shape[1]
    return pl.pallas_call(
        place_kernel,
        in_specs=[SMEM] + [VMEM] * 8,
        out_specs=[VMEM] * 2,
        out_shape=[jax.ShapeDtypeStruct((CHUNK, width), BF16)] * 2,
        compiler_params=pltpu.CompilerParams(**LIMIT),
    )(table, *pieces)


def half(value, core, after):
    def kernel(value, *refs):
        refs[-1][...] = value[pl.ds(core * 64, 64), :]

    return pl.pallas_call(
        kernel,
        in_specs=[VMEM] + [ANY] * len(after),
        out_specs=VMEM,
        out_shape=jax.ShapeDtypeStruct((64, value.shape[1]), BF16),
        compiler_params=pltpu.CompilerParams(**LIMIT),
    )(value, *after)


def share_kernel(count, *refs):
    pairs, outs = refs[: 2 * count], refs[2 * count :]
    first, rows = 0, 2 * UNIT
    for mine, theirs in zip(pairs[:count], pairs[count:]):
        for dx, out in enumerate(outs):
            total = mine[dx].astype(F32) + theirs[dx].astype(F32)
            out[pl.ds(first, rows), :] = total.reshape(rows, out.shape[1]).astype(out.dtype)
        first += rows


def share(mine, theirs):
    rows, width = len(mine) * 2 * UNIT, mine[0].shape[-1]
    return pl.pallas_call(
        lambda *refs: share_kernel(len(mine), *refs),
        in_specs=[VMEM] * (2 * len(mine)),
        out_specs=[VMEM] * 4,
        out_shape=[jax.ShapeDtypeStruct((rows, width), kind) for kind in (F32, BF16, BF16, BF16)],
        compiler_params=pltpu.CompilerParams(**LIMIT),
    )(*mine, *theirs)


def finish_kernel(table, *refs):
    terms, out = refs[:8], refs[8]
    for batch, steps in enumerate(SLOT_STEPS):
        own, *sent = terms[4 * batch : 4 * batch + 4]
        total = own[...]
        for block in sent:
            total = total + block[...].astype(F32)
        total = total.astype(BF16)
        for n, k in enumerate(steps):
            for chain in range(2):
                start = chain * 64 + lax.rem(table[10 - chain] + k, RING) * UNIT
                out[pl.ds(pl.multiple_of(start, UNIT), UNIT), :] = total[
                    (2 * n + chain) * UNIT : (2 * n + chain + 1) * UNIT
                ]


def finish(table, terms):
    return pl.pallas_call(
        finish_kernel,
        in_specs=[SMEM] + [VMEM] * 8,
        out_specs=VMEM,
        out_shape=jax.ShapeDtypeStruct((CHUNK, terms[0].shape[1]), BF16),
        compiler_params=pltpu.CompilerParams(**LIMIT),
    )(table, *terms)


def pass_on(both, received):
    def kernel(both, received, out):
        out[:CHUNK, :] = (both[:CHUNK, :].astype(F32) + received[...].astype(F32)).astype(BF16)

    return pl.pallas_call(
        kernel,
        in_specs=[VMEM] * 2,
        out_specs=VMEM,
        out_shape=jax.ShapeDtypeStruct(both.shape, BF16),
        input_output_aliases={0: 0},
        compiler_params=pltpu.CompilerParams(**LIMIT),
    )(both, received)


def blend_kernel(at, outs_parts, act, count, *refs):
    table, arrays, outs = refs[0], refs[1:count], refs[count:]
    height = 2 * UNIT

    def total_of(part):
        total = None
        for array, base, k in part:
            start = base
            if k is not None:
                start = pl.multiple_of(base + lax.rem(table[at] + k, RING) * height, height)
            value = arrays[array][pl.ds(start, height), :].astype(F32)
            total = value if total is None else total + value
        return total

    for parts, out in zip(outs_parts, outs):
        if act:
            gate, up = (total_of(part) for part in parts)
            out[...] = (gate / (1.0 + jnp.exp(-gate)) * up).astype(BF16)
        else:
            for m, part in enumerate(parts):
                out[pl.ds(m * height, height), :] = total_of(part).astype(BF16)


def blend(table, at, arrays, outs_parts, act=False):
    width = arrays[0].shape[1]
    count = 1 + len(arrays)
    heights = [2 * UNIT * (1 if act else len(parts)) for parts in outs_parts]
    return pl.pallas_call(
        lambda *refs: blend_kernel(at, outs_parts, act, count, *refs),
        in_specs=[SMEM] + [VMEM] * len(arrays),
        out_specs=[VMEM] * len(outs_parts),
        out_shape=[jax.ShapeDtypeStruct((height, width), BF16) for height in heights],
        compiler_params=pltpu.CompilerParams(**LIMIT),
    )(table, *arrays)


def body(tokens, gate_w, up_w, down_w):
    col, row = lax.axis_index("col"), lax.axis_index("row")
    z, y, x, core = col // RING, col % RING, row // 2, row % 2
    table = [2 * ((x - b // 2) % RING) + b % 2 for b in range(8)] + [core, z, y]
    table = jnp.stack(table).astype(jnp.int32)

    exchanged = []
    first_rows, later_rows = pick(table, tokens)
    for mine in (first_rows, later_rows):
        mine = mine.reshape(-1, UNIT, mine.shape[1])
        same = jnp.stack([mine, chip_send(mine, 1), chip_send(mine, 2), chip_send(mine, -1)])
        exchanged.append((same, core_swap(same)))
    quarters, rest = exchanged

    far = up_gate(quarters, 0, [[(0, 0), (1, 0)], [(2, 0), (3, 0)]], table, gate_w, up_w)
    routes = [("y", 1), ("y", -1), ("z", 1), ("z", -1)]
    first = [ring_send(value, *route) for value, route in zip(far, routes)]
    beside = up_gate(
        rest, 0, [[(0, 0), (0, 1)], [(1, 1), (1, 0)], [(2, 0), (2, 1)], [(3, 1), (3, 0)]], table, gate_w, up_w
    )
    passed = [pass_on(both, value) for both, value in zip(beside, first)]
    second = [ring_send(value, *route) for value, route in zip(passed, routes)]
    near = up_gate(rest, 4, [[(0, 0), (1, 0)], [(2, 0), (3, 0)]], table, gate_w, up_w, after=passed)

    hidden = []
    gate = lambda k: [(0, 0, k), (2, 0, k), (3, CHUNK, k)]
    up = lambda k: [(1, 0, k), (3, 0, k), (2, CHUNK, k)]
    for chain, (axis, at) in enumerate((("z", 9), ("y", 10))):
        arrays = [*near[2 * chain : 2 * chain + 2], *second[2 * chain : 2 * chain + 2]]
        ahead, behind = blend(table, at, arrays, [[gate(2), up(1)], [up(2), gate(3)]])
        arrays += [ring_send(ahead, axis, 1), ring_send(behind, axis, -1)]
        more, less = blend(
            table, at, arrays, [[gate(1) + [(4, 0, None)]], [up(3) + [(5, 0, None)]]]
        )
        arrays += [ring_send(more, axis, 1), ring_send(less, axis, -1)]
        block = 2 * UNIT
        terms = [gate(0) + [(5, block, None), (6, 0, None)], up(0) + [(4, block, None), (7, 0, None)]]
        hidden += blend(table, at, arrays, [terms], act=True)

    pieces = []
    for value, axis in zip(hidden, ("z", "y")):
        pieces += [value, ring_send(value, axis, -1), ring_send(value, axis, 2), ring_send(value, axis, 1)]
    own = place(table, pieces)

    behind = [ring_send(value, axis, 1) for value, axis in zip(own, "yz")]
    ahead = [ring_send(value, axis, -1) for value, axis in zip(own, "yz")]
    sums = down(table, 1, own, down_w)
    onward = [(half(b, 0, sums[0]), half(a, 1, sums[0])) for b, a in zip(behind, ahead)]
    distant = []
    for (forward, backward), axis in zip(onward, "yz"):
        distant += [ring_send(forward, axis, 1), ring_send(backward, axis, -1)]
    sums += down(table, 2, [*behind, *ahead], down_w, after=[*onward[0], *onward[1]])

    terms, sent = [], []
    for batch in range(2):
        if batch == 1:
            sums = down(table, 1, distant, down_w, after=())
        own_total, *sent = share([mine for mine, other in sums], [core_swap(other) for mine, other in sums])
        terms += [own_total] + [chip_send(value, step) for value, step in zip(sent, (-1, 2, 1))]
    return finish(table, terms)


def solution(mesh):
    placed = (P("row", "col"), P("col", "row"), P("col", "row"), P("row", "col"))
    return jax.shard_map(
        body, mesh=mesh, in_specs=placed, out_specs=P("row", "col"), check_vma=False
    )
```

```python
import jax
import jax.numpy as jnp
from jax import lax
from jax.experimental import pallas as pl
from jax.experimental.pallas import tpu as pltpu
from jax.sharding import PartitionSpec as P

BF16, F32 = jnp.bfloat16, jnp.float32
RING = 4
UNIT = 16
CHUNK = 8 * UNIT
SLOT_STEPS = ((0, 3), (1, 2))
LIMIT = dict(vmem_limit_bytes=14 * 1024 * 1024)
VMEM, ANY = pl.BlockSpec(memory_space=pltpu.VMEM), pl.BlockSpec(memory_space=pl.ANY)
SMEM = pl.BlockSpec(memory_space=pltpu.SMEM)


def chip_send(value, step):
    pairs = [(2 * x + c, 2 * ((x + step) % RING) + c) for x in range(RING) for c in range(2)]
    return lax.ppermute(value, "row", pairs)


def core_swap(value):
    return lax.ppermute(value, "row", [(r, r ^ 1) for r in range(2 * RING)])


def ring_send(value, axis, step):
    pairs = []
    for z in range(RING):
        for y in range(RING):
            to_z, to_y = (z, (y + step) % RING) if axis == "y" else ((z + step) % RING, y)
            pairs.append((RING * z + y, RING * to_z + to_y))
    return lax.ppermute(value, "col", pairs)


def preload(weights, after):
    count, parts = len(weights), 4

    def kernel(*refs):
        sources, outs, sems = refs[:count], refs[-1 - count : -1], refs[-1]
        copies = []
        for m in range(count):
            rows = sources[m].shape[0] // parts
            for n in range(parts):
                block = pl.ds(n * rows, rows)
                copies.append(
                    pltpu.make_async_copy(sources[m].at[block], outs[m].at[block], sems.at[m * parts + n])
                )
        for copy in copies:
            copy.start()
        for copy in copies:
            copy.wait()

    return pl.pallas_call(
        kernel,
        in_specs=[ANY] * (count + len(after)),
        out_specs=[VMEM] * count,
        out_shape=[jax.ShapeDtypeStruct(weight.shape, BF16) for weight in weights],
        scratch_shapes=[pltpu.SemaphoreType.DMA((count * parts,))],
        compiler_params=pltpu.CompilerParams(vmem_limit_bytes=38 * 1024 * 1024),
        cost_estimate=pl.CostEstimate(
            flops=0, bytes_accessed=4 * sum(weight.size for weight in weights), transcendentals=0
        ),
    )(*weights, *after)


def tile_cuts(size):
    step = size // 1024 * 256
    return [(n * step, step) for n in range(3)] + [(3 * step, size - 3 * step)]


def pick(table, tokens, places, after=()):
    depth = tokens.shape[1]

    def kernel(table, tokens, *refs):
        for n, (chain, k) in enumerate(places):
            start = chain * 64 + lax.rem(table[10 - chain] + k, RING) * UNIT
            refs[-1][n] = tokens[pl.ds(pl.multiple_of(start, UNIT), UNIT), :]

    return pl.pallas_call(
        kernel,
        in_specs=[SMEM, VMEM] + [ANY] * len(after),
        out_specs=VMEM,
        out_shape=jax.ShapeDtypeStruct((len(places), UNIT, depth), BF16),
        compiler_params=pltpu.CompilerParams(**LIMIT),
    )(table, tokens, *after)


def stacked(values, after):
    def kernel(*refs):
        for n in range(len(values)):
            refs[-1][n] = refs[n][...]

    return pl.pallas_call(
        kernel,
        in_specs=[VMEM] * len(values) + [ANY] * len(after),
        out_specs=VMEM,
        out_shape=jax.ShapeDtypeStruct((len(values),) + values[0].shape, BF16),
        compiler_params=pltpu.CompilerParams(**LIMIT),
    )(*values, *after)


def up_gate_kernel(first, layout, count, *refs):
    chunks = len(layout)
    table, gate_w, up_w = refs[:3]
    halves = refs[3:5]
    outs, rows = refs[count:-1], refs[-1]
    width = gate_w.shape[1]
    for n, half in enumerate(halves):
        core = table[8] if n == 0 else 1 - table[8]
        for dx in range(RING):
            for c in range(chunks):
                start = pl.multiple_of(c * CHUNK + 2 * dx * UNIT + core * UNIT, UNIT)
                rows[pl.ds(start, UNIT), :] = half[dx, first + c]
    for kind, weight in enumerate((gate_w, up_w)):
        for start, size in tile_cuts(width):
            value = jnp.dot(
                rows[...], weight[:, start : start + size], preferred_element_type=F32
            ).astype(BF16)
            for c in range(chunks):
                out, block = layout[c][kind]
                outs[out][pl.ds(block * CHUNK, CHUNK), pl.ds(start, size)] = value[
                    c * CHUNK : (c + 1) * CHUNK
                ]


def up_gate(halves, first, layout, table, gate_w, up_w, after=()):
    depth, width = gate_w.shape
    chunks = len(layout)
    places = [place for pair in layout for place in pair]
    outs = 1 + max(place[0] for place in places)
    shape = (CHUNK * (1 + max(place[1] for place in places)), width)
    operands = [table, gate_w, up_w, *halves, *after]
    return pl.pallas_call(
        lambda *refs: up_gate_kernel(first, layout, len(operands), *refs),
        in_specs=[SMEM] + [VMEM] * 4 + [ANY] * len(after),
        out_specs=[VMEM] * outs,
        out_shape=[jax.ShapeDtypeStruct(shape, BF16)] * outs,
        scratch_shapes=[pltpu.VMEM((chunks * CHUNK, depth), BF16)],
        compiler_params=pltpu.CompilerParams(**LIMIT),
        cost_estimate=pl.CostEstimate(
            flops=4 * chunks * CHUNK * depth * width,
            bytes_accessed=4 * depth * width + chunks * CHUNK * (depth + 2 * width) * 2,
            transcendentals=0,
        ),
    )(*operands)


def down_kernel(count, slots, *refs):
    table, weight = refs[:2]
    pieces = refs[2 : 2 + count]
    outs, (rows, stage) = refs[-2 - 2 * slots : -2], refs[-2:]
    core = table[8]
    height = rows.shape[0] // count
    for n, piece in enumerate(pieces):
        rows[pl.ds(n * height, height), :] = piece[...]
    for start, size in tile_cuts(weight.shape[1]):
        part = jnp.dot(rows[...], weight[:, start : start + size], preferred_element_type=F32)
        part = part.astype(BF16).reshape(slots, 2, 2, RING, UNIT, size)
        for s in range(slots):
            for chain in range(2):
                for c in range(2):
                    for dx in range(RING):
                        stage[c, s, dx, chain, :, pl.ds(start, size)] = part[s, chain, c, dx]
    for s in range(slots):
        outs[2 * s][...] = stage[core, s]
        outs[2 * s + 1][...] = stage[1 - core, s]


def down(table, slots, pieces, weight, after=()):
    depth, width = weight.shape
    tokens = 2 * CHUNK * slots
    shape = (RING, 2, UNIT, width)
    operands = [table, weight, *pieces, *after]
    outs = pl.pallas_call(
        lambda *refs: down_kernel(len(pieces), slots, *refs),
        in_specs=[SMEM] + [VMEM] * (1 + len(pieces)) + [ANY] * len(after),
        out_specs=[VMEM] * (2 * slots),
        out_shape=[jax.ShapeDtypeStruct(shape, BF16)] * (2 * slots),
        scratch_shapes=[pltpu.VMEM((tokens, depth), BF16), pltpu.VMEM((2, slots) + shape, BF16)],
        compiler_params=pltpu.CompilerParams(**LIMIT),
        cost_estimate=pl.CostEstimate(
            flops=2 * tokens * depth * width,
            bytes_accessed=2 * (depth * width + tokens * (depth + width)),
            transcendentals=0,
        ),
    )(*operands)
    return [(outs[2 * s], outs[2 * s + 1]) for s in range(slots)]


def place_kernel(table, *refs):
    pieces, outs = refs[:8], refs[8:]
    for chain in range(2):
        for k in range(RING):
            start = lax.rem(table[9 + chain] + k, RING) * UNIT
            for core in range(2):
                outs[chain][pl.ds(pl.multiple_of(start + core * 64, UNIT), UNIT), :] = pieces[4 * chain + k][
                    pl.ds(core * UNIT, UNIT), :
                ]


def place(table, pieces):
    width = pieces[0].shape[1]
    return pl.pallas_call(
        place_kernel,
        in_specs=[SMEM] + [VMEM] * 8,
        out_specs=[VMEM] * 2,
        out_shape=[jax.ShapeDtypeStruct((CHUNK, width), BF16)] * 2,
        compiler_params=pltpu.CompilerParams(**LIMIT),
    )(table, *pieces)


def half(value, core, after):
    def kernel(value, *refs):
        refs[-1][...] = value[pl.ds(core * 64, 64), :]

    return pl.pallas_call(
        kernel,
        in_specs=[VMEM] + [ANY] * len(after),
        out_specs=VMEM,
        out_shape=jax.ShapeDtypeStruct((64, value.shape[1]), BF16),
        compiler_params=pltpu.CompilerParams(**LIMIT),
    )(value, *after)


def share_kernel(count, *refs):
    pairs, outs = refs[: 2 * count], refs[2 * count :]
    first, rows = 0, 2 * UNIT
    for mine, theirs in zip(pairs[:count], pairs[count:]):
        for dx, out in enumerate(outs):
            total = mine[dx].astype(F32) + theirs[dx].astype(F32)
            out[pl.ds(first, rows), :] = total.reshape(rows, out.shape[1]).astype(out.dtype)
        first += rows


def share(mine, theirs):
    rows, width = len(mine) * 2 * UNIT, mine[0].shape[-1]
    return pl.pallas_call(
        lambda *refs: share_kernel(len(mine), *refs),
        in_specs=[VMEM] * (2 * len(mine)),
        out_specs=[VMEM] * 4,
        out_shape=[jax.ShapeDtypeStruct((rows, width), kind) for kind in (F32, BF16, BF16, BF16)],
        compiler_params=pltpu.CompilerParams(**LIMIT),
    )(*mine, *theirs)


def finish_kernel(table, *refs):
    terms, out = refs[:8], refs[8]
    for batch, steps in enumerate(SLOT_STEPS):
        own, *sent = terms[4 * batch : 4 * batch + 4]
        total = own[...]
        for block in sent:
            total = total + block[...].astype(F32)
        total = total.astype(BF16)
        for n, k in enumerate(steps):
            for chain in range(2):
                start = chain * 64 + lax.rem(table[10 - chain] + k, RING) * UNIT
                out[pl.ds(pl.multiple_of(start, UNIT), UNIT), :] = total[
                    (2 * n + chain) * UNIT : (2 * n + chain + 1) * UNIT
                ]


def finish(table, terms):
    return pl.pallas_call(
        finish_kernel,
        in_specs=[SMEM] + [VMEM] * 8,
        out_specs=VMEM,
        out_shape=jax.ShapeDtypeStruct((CHUNK, terms[0].shape[1]), BF16),
        compiler_params=pltpu.CompilerParams(**LIMIT),
    )(table, *terms)


def pass_on(both, received):
    def kernel(both, received, out):
        out[:CHUNK, :] = (both[:CHUNK, :].astype(F32) + received[...].astype(F32)).astype(BF16)

    return pl.pallas_call(
        kernel,
        in_specs=[VMEM] * 2,
        out_specs=VMEM,
        out_shape=jax.ShapeDtypeStruct(both.shape, BF16),
        input_output_aliases={0: 0},
        compiler_params=pltpu.CompilerParams(**LIMIT),
    )(both, received)


def blend_kernel(at, outs_parts, act, count, *refs):
    table, arrays, outs = refs[0], refs[1:count], refs[count:]
    height = 2 * UNIT

    def total_of(part):
        total = None
        for array, base, k in part:
            start = base
            if k is not None:
                start = pl.multiple_of(base + lax.rem(table[at] + k, RING) * height, height)
            value = arrays[array][pl.ds(start, height), :].astype(F32)
            total = value if total is None else total + value
        return total

    for parts, out in zip(outs_parts, outs):
        if act:
            gate, up = (total_of(part) for part in parts)
            out[...] = (gate / (1.0 + jnp.exp(-gate)) * up).astype(BF16)
        else:
            for m, part in enumerate(parts):
                out[pl.ds(m * height, height), :] = total_of(part).astype(BF16)


def blend(table, at, arrays, outs_parts, act=False):
    width = arrays[0].shape[1]
    count = 1 + len(arrays)
    heights = [2 * UNIT * (1 if act else len(parts)) for parts in outs_parts]
    return pl.pallas_call(
        lambda *refs: blend_kernel(at, outs_parts, act, count, *refs),
        in_specs=[SMEM] + [VMEM] * len(arrays),
        out_specs=[VMEM] * len(outs_parts),
        out_shape=[jax.ShapeDtypeStruct((height, width), BF16) for height in heights],
        compiler_params=pltpu.CompilerParams(**LIMIT),
    )(table, *arrays)


def body(tokens, gate_w, up_w, down_w):
    col, row = lax.axis_index("col"), lax.axis_index("row")
    z, y, x, core = col // RING, col % RING, row // 2, row % 2
    table = [2 * ((x - b // 2) % RING) + b % 2 for b in range(8)] + [core, z, y]
    table = jnp.stack(table).astype(jnp.int32)

    def other_chips(mine):
        return [mine, chip_send(mine, 1), chip_send(mine, 2), chip_send(mine, -1)]

    quarters = other_chips(pick(table, tokens, ((0, 2), (1, 2))))
    gate_w, up_w = preload((gate_w, up_w), after=quarters[:1])
    quarters = stacked(quarters, after=[gate_w])
    rest = other_chips(pick(table, tokens, ((0, 1), (0, 3), (1, 1), (1, 3)), after=[quarters]))

    far = up_gate(
        (quarters, core_swap(quarters)), 0, [[(0, 0), (1, 0)], [(2, 0), (3, 0)]], table, gate_w, up_w
    )
    rest = stacked(rest, after=far[:1])
    rest = (rest, core_swap(rest))
    routes = [("y", 1), ("y", -1), ("z", 1), ("z", -1)]
    first = [ring_send(value, *route) for value, route in zip(far, routes)]
    beside = up_gate(
        rest, 0, [[(0, 0), (0, 1)], [(1, 1), (1, 0)], [(2, 0), (2, 1)], [(3, 1), (3, 0)]], table, gate_w, up_w
    )
    passed = [pass_on(both, value) for both, value in zip(beside, first)]
    second = [ring_send(value, *route) for value, route in zip(passed, routes)]
    rest = stacked(other_chips(pick(table, tokens, ((0, 0), (1, 0)), after=passed)), after=[])
    rest = (rest, core_swap(rest))
    near = up_gate(rest, 0, [[(0, 0), (1, 0)], [(2, 0), (3, 0)]], table, gate_w, up_w, after=passed)

    hidden = []
    gate = lambda k: [(0, 0, k), (2, 0, k), (3, CHUNK, k)]
    up = lambda k: [(1, 0, k), (3, 0, k), (2, CHUNK, k)]
    for chain, (axis, at) in enumerate((("z", 9), ("y", 10))):
        arrays = [*near[2 * chain : 2 * chain + 2], *second[2 * chain : 2 * chain + 2]]
        ahead, behind = blend(table, at, arrays, [[gate(2), up(1)], [up(2), gate(3)]])
        arrays += [ring_send(ahead, axis, 1), ring_send(behind, axis, -1)]
        more, less = blend(
            table, at, arrays, [[gate(1) + [(4, 0, None)]], [up(3) + [(5, 0, None)]]]
        )
        arrays += [ring_send(more, axis, 1), ring_send(less, axis, -1)]
        block = 2 * UNIT
        terms = [gate(0) + [(5, block, None), (6, 0, None)], up(0) + [(4, block, None), (7, 0, None)]]
        hidden += blend(table, at, arrays, [terms], act=True)

    pieces = []
    for value, axis in zip(hidden, ("z", "y")):
        pieces += [value, ring_send(value, axis, -1), ring_send(value, axis, 2), ring_send(value, axis, 1)]
    own = place(table, pieces)

    behind = [ring_send(value, axis, 1) for value, axis in zip(own, "yz")]
    ahead = [ring_send(value, axis, -1) for value, axis in zip(own, "yz")]
    near_sum = down(table, 1, own, down_w)[0]
    near_theirs = core_swap(near_sum[1])
    onward = [(half(b, 0, [near_theirs]), half(a, 1, [near_theirs])) for b, a in zip(behind, ahead)]
    distant = []
    for (forward, backward), axis in zip(onward, "yz"):
        distant += [ring_send(forward, axis, 1), ring_send(backward, axis, -1)]
    behind_sum, ahead_sum = (
        down(table, 1, pieces, down_w, after=[*onward[0], *onward[1]])[0] for pieces in (behind, ahead)
    )

    def spread(sums, theirs):
        own_total, *sent = share([mine for mine, other in sums], theirs)
        return sent, [own_total] + [chip_send(value, step) for value, step in zip(sent, (-1, 2, 1))]

    sent, terms = spread([near_sum, behind_sum], [near_theirs, core_swap(behind_sum[1])])
    last_sum = down(table, 1, distant, down_w, after=sent)[0]
    _, more_terms = spread([ahead_sum, last_sum], [core_swap(ahead_sum[1]), core_swap(last_sum[1])])
    return finish(table, terms + more_terms)


def solution(mesh):
    placed = (P("row", "col"), P("col", "row"), P("col", "row"), P("row", "col"))
    return jax.shard_map(
        body, mesh=mesh, in_specs=placed, out_specs=P("row", "col"), check_vma=False
    )
```

```python
import jax
import jax.numpy as jnp
from jax import lax
from jax.experimental import pallas as pl
from jax.experimental.pallas import tpu as pltpu
from jax.sharding import PartitionSpec as P

BF16, F32 = jnp.bfloat16, jnp.float32
RING = 4
UNIT = 16
CHUNK = 8 * UNIT
LIMIT = dict(vmem_limit_bytes=14 * 1024 * 1024)
VMEM, ANY = pl.BlockSpec(memory_space=pltpu.VMEM), pl.BlockSpec(memory_space=pl.ANY)
SMEM = pl.BlockSpec(memory_space=pltpu.SMEM)


def chip_send(value, step):
    pairs = [(2 * x + c, 2 * ((x + step) % RING) + c) for x in range(RING) for c in range(2)]
    return lax.ppermute(value, "row", pairs)


def core_swap(value):
    return lax.ppermute(value, "row", [(r, r ^ 1) for r in range(2 * RING)])


def ring_send(value, axis, step):
    pairs = []
    for z in range(RING):
        for y in range(RING):
            to_z, to_y = (z, (y + step) % RING) if axis == "y" else ((z + step) % RING, y)
            pairs.append((RING * z + y, RING * to_z + to_y))
    return lax.ppermute(value, "col", pairs)


def preload(weights, after):
    count, parts = len(weights), 4

    def kernel(*refs):
        sources, outs, sems = refs[:count], refs[-1 - count : -1], refs[-1]
        copies = []
        for m in range(count):
            rows = sources[m].shape[0] // parts
            for n in range(parts):
                block = pl.ds(n * rows, rows)
                copies.append(
                    pltpu.make_async_copy(sources[m].at[block], outs[m].at[block], sems.at[m * parts + n])
                )
        for copy in copies:
            copy.start()
        for copy in copies:
            copy.wait()

    return pl.pallas_call(
        kernel,
        in_specs=[ANY] * (count + len(after)),
        out_specs=[VMEM] * count,
        out_shape=[jax.ShapeDtypeStruct(weight.shape, BF16) for weight in weights],
        scratch_shapes=[pltpu.SemaphoreType.DMA((count * parts,))],
        compiler_params=pltpu.CompilerParams(vmem_limit_bytes=38 * 1024 * 1024),
        cost_estimate=pl.CostEstimate(
            flops=0, bytes_accessed=4 * sum(weight.size for weight in weights), transcendentals=0
        ),
    )(*weights, *after)


def tile_cuts(size):
    step = size // 1024 * 256
    return [(n * step, step) for n in range(3)] + [(3 * step, size - 3 * step)]


def pick(table, tokens, groups):
    depth = tokens.shape[1]

    def kernel(table, tokens, *outs):
        for places, out in zip(groups, outs):
            for n, (chain, k) in enumerate(places):
                start = chain * 64 + lax.rem(table[10 - chain] + k, RING) * UNIT
                out[n] = tokens[pl.ds(pl.multiple_of(start, UNIT), UNIT), :]

    return pl.pallas_call(
        kernel,
        in_specs=[SMEM, VMEM],
        out_specs=[VMEM] * len(groups),
        out_shape=[jax.ShapeDtypeStruct((len(places), UNIT, depth), BF16) for places in groups],
        compiler_params=pltpu.CompilerParams(**LIMIT),
    )(table, tokens)


def behind_of(value, after):
    return pl.pallas_call(
        lambda *refs: None,
        in_specs=[ANY] * (1 + len(after)),
        out_specs=ANY,
        out_shape=jax.ShapeDtypeStruct(value.shape, value.dtype),
        input_output_aliases={0: 0},
        compiler_params=pltpu.CompilerParams(**LIMIT),
    )(value, *after)


def stacked(values, after):
    def kernel(*refs):
        for n in range(len(values)):
            refs[-1][n] = refs[n][...]

    return pl.pallas_call(
        kernel,
        in_specs=[VMEM] * len(values) + [ANY] * len(after),
        out_specs=VMEM,
        out_shape=jax.ShapeDtypeStruct((len(values),) + values[0].shape, BF16),
        compiler_params=pltpu.CompilerParams(**LIMIT),
    )(*values, *after)


def up_gate_kernel(first, layout, count, *refs):
    chunks = len(layout)
    table, gate_w, up_w = refs[:3]
    halves = refs[3:5]
    outs, rows = refs[count:-1], refs[-1]
    width = gate_w.shape[1]
    for n, half in enumerate(halves):
        core = table[8] if n == 0 else 1 - table[8]
        for dx in range(RING):
            for c in range(chunks):
                start = pl.multiple_of(c * CHUNK + 2 * dx * UNIT + core * UNIT, UNIT)
                rows[pl.ds(start, UNIT), :] = half[dx, first + c]
    for kind, weight in enumerate((gate_w, up_w)):
        for start, size in tile_cuts(width):
            value = jnp.dot(
                rows[...], weight[:, start : start + size], preferred_element_type=F32
            ).astype(BF16)
            for c in range(chunks):
                out, block = layout[c][kind]
                outs[out][pl.ds(block * CHUNK, CHUNK), pl.ds(start, size)] = value[
                    c * CHUNK : (c + 1) * CHUNK
                ]


def up_gate(halves, first, layout, table, gate_w, up_w, after=()):
    depth, width = gate_w.shape
    chunks = len(layout)
    places = [place for pair in layout for place in pair]
    outs = 1 + max(place[0] for place in places)
    shape = (CHUNK * (1 + max(place[1] for place in places)), width)
    operands = [table, gate_w, up_w, *halves, *after]
    return pl.pallas_call(
        lambda *refs: up_gate_kernel(first, layout, len(operands), *refs),
        in_specs=[SMEM] + [VMEM] * 4 + [ANY] * len(after),
        out_specs=[VMEM] * outs,
        out_shape=[jax.ShapeDtypeStruct(shape, BF16)] * outs,
        scratch_shapes=[pltpu.VMEM((chunks * CHUNK, depth), BF16)],
        compiler_params=pltpu.CompilerParams(**LIMIT),
        cost_estimate=pl.CostEstimate(
            flops=4 * chunks * CHUNK * depth * width,
            bytes_accessed=4 * depth * width + chunks * CHUNK * (depth + 2 * width) * 2,
            transcendentals=0,
        ),
    )(*operands)


def down_kernel(count, slots, *refs):
    table, weight = refs[:2]
    pieces = refs[2 : 2 + count]
    outs, (rows, stage) = refs[-2 - 2 * slots : -2], refs[-2:]
    core = table[8]
    height = rows.shape[0] // count
    for n, piece in enumerate(pieces):
        rows[pl.ds(n * height, height), :] = piece[...]
    for start, size in tile_cuts(weight.shape[1]):
        part = jnp.dot(rows[...], weight[:, start : start + size], preferred_element_type=F32)
        part = part.astype(BF16).reshape(slots, 2, 2, RING, UNIT, size)
        for s in range(slots):
            for chain in range(2):
                for c in range(2):
                    for dx in range(RING):
                        stage[c, s, dx, chain, :, pl.ds(start, size)] = part[s, chain, c, dx]
    for s in range(slots):
        outs[2 * s][...] = stage[core, s]
        outs[2 * s + 1][...] = stage[1 - core, s]


def down(table, slots, pieces, weight, after=()):
    depth, width = weight.shape
    tokens = 2 * CHUNK * slots
    shape = (RING, 2, UNIT, width)
    operands = [table, weight, *pieces, *after]
    outs = pl.pallas_call(
        lambda *refs: down_kernel(len(pieces), slots, *refs),
        in_specs=[SMEM] + [VMEM] * (1 + len(pieces)) + [ANY] * len(after),
        out_specs=[VMEM] * (2 * slots),
        out_shape=[jax.ShapeDtypeStruct(shape, BF16)] * (2 * slots),
        scratch_shapes=[pltpu.VMEM((tokens, depth), BF16), pltpu.VMEM((2, slots) + shape, BF16)],
        compiler_params=pltpu.CompilerParams(**LIMIT),
        cost_estimate=pl.CostEstimate(
            flops=2 * tokens * depth * width,
            bytes_accessed=2 * (depth * width + tokens * (depth + width)),
            transcendentals=0,
        ),
    )(*operands)
    return [(outs[2 * s], outs[2 * s + 1]) for s in range(slots)]


def place_kernel(table, *refs):
    pieces, outs = refs[:8], refs[8:]
    for chain in range(2):
        for k in range(RING):
            start = lax.rem(table[9 + chain] + k, RING) * UNIT
            for core in range(2):
                outs[chain][pl.ds(pl.multiple_of(start + core * 64, UNIT), UNIT), :] = pieces[4 * chain + k][
                    pl.ds(core * UNIT, UNIT), :
                ]


def place(table, pieces):
    width = pieces[0].shape[1]
    return pl.pallas_call(
        place_kernel,
        in_specs=[SMEM] + [VMEM] * 8,
        out_specs=[VMEM] * 2,
        out_shape=[jax.ShapeDtypeStruct((CHUNK, width), BF16)] * 2,
        compiler_params=pltpu.CompilerParams(**LIMIT),
    )(table, *pieces)


def half(value, core, after):
    def kernel(value, *refs):
        refs[-1][...] = value[pl.ds(core * 64, 64), :]

    return pl.pallas_call(
        kernel,
        in_specs=[VMEM] + [ANY] * len(after),
        out_specs=VMEM,
        out_shape=jax.ShapeDtypeStruct((64, value.shape[1]), BF16),
        compiler_params=pltpu.CompilerParams(**LIMIT),
    )(value, *after)


def share(mine, theirs):
    def kernel(mine, theirs, *outs):
        for dx, out in enumerate(outs):
            total = mine[dx].astype(F32) + theirs[dx].astype(F32)
            out[...] = total.reshape(out.shape).astype(out.dtype)

    shape = (2 * UNIT, mine.shape[-1])
    return pl.pallas_call(
        kernel,
        in_specs=[VMEM] * 2,
        out_specs=[VMEM] * 4,
        out_shape=[jax.ShapeDtypeStruct(shape, kind) for kind in (F32, BF16, BF16, BF16)],
        compiler_params=pltpu.CompilerParams(**LIMIT),
    )(mine, theirs)


def finish(table, slots):
    arrays = [array for _, terms in slots for array, _ in terms]

    def kernel(table, *refs):
        sources, out = iter(refs[:-1]), refs[-1]
        for k, terms in slots:
            total = None
            for _, first in terms:
                value = next(sources)[pl.ds(first, 2 * UNIT), :].astype(F32)
                total = value if total is None else total + value
            total = total.astype(BF16)
            for chain in range(2):
                start = chain * 64 + lax.rem(table[10 - chain] + k, RING) * UNIT
                out[pl.ds(pl.multiple_of(start, UNIT), UNIT), :] = total[chain * UNIT : (chain + 1) * UNIT]

    return pl.pallas_call(
        kernel,
        in_specs=[SMEM] + [VMEM] * len(arrays),
        out_specs=VMEM,
        out_shape=jax.ShapeDtypeStruct((CHUNK, arrays[0].shape[1]), BF16),
        compiler_params=pltpu.CompilerParams(**LIMIT),
    )(table, *arrays)


def pass_on(both, received):
    def kernel(both, received, out):
        out[:CHUNK, :] = (both[:CHUNK, :].astype(F32) + received[...].astype(F32)).astype(BF16)

    return pl.pallas_call(
        kernel,
        in_specs=[VMEM] * 2,
        out_specs=VMEM,
        out_shape=jax.ShapeDtypeStruct(both.shape, BF16),
        input_output_aliases={0: 0},
        compiler_params=pltpu.CompilerParams(**LIMIT),
    )(both, received)


def blend_kernel(at, outs_parts, act, count, *refs):
    table, arrays, outs = refs[0], refs[1:count], refs[count:]
    height = 2 * UNIT

    def total_of(part):
        total = None
        for array, base, k in part:
            start = base
            if k is not None:
                start = pl.multiple_of(base + lax.rem(table[at] + k, RING) * height, height)
            value = arrays[array][pl.ds(start, height), :].astype(F32)
            total = value if total is None else total + value
        return total

    for parts, out in zip(outs_parts, outs):
        if act:
            gate, up = (total_of(part) for part in parts)
            out[...] = (gate / (1.0 + jnp.exp(-gate)) * up).astype(BF16)
        else:
            for m, part in enumerate(parts):
                out[pl.ds(m * height, height), :] = total_of(part).astype(BF16)


def blend(table, at, arrays, outs_parts, act=False):
    width = arrays[0].shape[1]
    count = 1 + len(arrays)
    heights = [2 * UNIT * (1 if act else len(parts)) for parts in outs_parts]
    return pl.pallas_call(
        lambda *refs: blend_kernel(at, outs_parts, act, count, *refs),
        in_specs=[SMEM] + [VMEM] * len(arrays),
        out_specs=[VMEM] * len(outs_parts),
        out_shape=[jax.ShapeDtypeStruct((height, width), BF16) for height in heights],
        compiler_params=pltpu.CompilerParams(**LIMIT),
    )(table, *arrays)


def body(tokens, gate_w, up_w, down_w):
    col, row = lax.axis_index("col"), lax.axis_index("row")
    z, y, x, core = col // RING, col % RING, row // 2, row % 2
    table = [2 * ((x - b // 2) % RING) + b % 2 for b in range(8)] + [core, z, y]
    table = jnp.stack(table).astype(jnp.int32)

    def other_chips(mine):
        return [mine, chip_send(mine, 1), chip_send(mine, 2), chip_send(mine, -1)]

    groups = (((0, 2), (1, 2)), ((0, 1), (0, 3), (1, 1), (1, 3)), ((0, 0), (1, 0)))
    far_rows, beside_rows, near_rows = pick(table, tokens, groups)
    quarters = other_chips(far_rows)
    gate_w, up_w = preload((gate_w, up_w), after=quarters[:1])
    quarters = stacked(quarters, after=[gate_w])
    rest = other_chips(behind_of(beside_rows, [quarters]))

    far = up_gate(
        (quarters, core_swap(quarters)), 0, [[(0, 0), (1, 0)], [(2, 0), (3, 0)]], table, gate_w, up_w
    )
    rest = stacked(rest, after=far[:1])
    rest = (rest, core_swap(rest))
    routes = [("y", 1), ("y", -1), ("z", 1), ("z", -1)]
    first = [ring_send(value, *route) for value, route in zip(far, routes)]
    beside = up_gate(
        rest, 0, [[(0, 0), (0, 1)], [(1, 1), (1, 0)], [(2, 0), (2, 1)], [(3, 1), (3, 0)]], table, gate_w, up_w
    )
    passed = [pass_on(both, value) for both, value in zip(beside, first)]
    second = [ring_send(value, *route) for value, route in zip(passed, routes)]
    rest = stacked(other_chips(behind_of(near_rows, passed)), after=[])
    rest = (rest, core_swap(rest))
    near = up_gate(rest, 0, [[(0, 0), (1, 0)], [(2, 0), (3, 0)]], table, gate_w, up_w, after=passed)

    hidden = []
    gate = lambda k: [(0, 0, k), (2, 0, k), (3, CHUNK, k)]
    up = lambda k: [(1, 0, k), (3, 0, k), (2, CHUNK, k)]
    for chain, (axis, at) in enumerate((("z", 9), ("y", 10))):
        arrays = [*near[2 * chain : 2 * chain + 2], *second[2 * chain : 2 * chain + 2]]
        ahead, behind = blend(table, at, arrays, [[gate(2), up(1)], [up(2), gate(3)]])
        arrays += [ring_send(ahead, axis, 1), ring_send(behind, axis, -1)]
        more, less = blend(
            table, at, arrays, [[gate(1) + [(4, 0, None)]], [up(3) + [(5, 0, None)]]]
        )
        arrays += [ring_send(more, axis, 1), ring_send(less, axis, -1)]
        block = 2 * UNIT
        terms = [gate(0) + [(5, block, None), (6, 0, None)], up(0) + [(4, block, None), (7, 0, None)]]
        hidden += blend(table, at, arrays, [terms], act=True)

    pieces = []
    for value, axis in zip(hidden, ("z", "y")):
        pieces += [value, ring_send(value, axis, -1), ring_send(value, axis, 2), ring_send(value, axis, 1)]
    own = place(table, pieces)

    behind = [ring_send(value, axis, 1) for value, axis in zip(own, "yz")]
    ahead = [ring_send(value, axis, -1) for value, axis in zip(own, "yz")]
    near_sum = down(table, 1, own, down_w)[0]
    near_parts = share(near_sum[0], core_swap(near_sum[1]))
    near_two = chip_send(near_parts[2], 2)
    onward = [(half(b, 0, [near_two]), half(a, 1, [near_two])) for b, a in zip(behind, ahead)]
    distant = []
    for (forward, backward), axis in zip(onward, "yz"):
        distant += [ring_send(forward, axis, 1), ring_send(backward, axis, -1)]
    behind_sum, ahead_sum = (
        down(table, 1, pieces, down_w, after=[*onward[0], *onward[1]])[0] for pieces in (behind, ahead)
    )
    behind_parts = share(behind_sum[0], core_swap(behind_sum[1]))
    last_sum = down(table, 1, distant, down_w, after=behind_parts)[0]

    def both_sent(one, two, dx, step):
        return chip_send(jnp.concatenate([one[dx], two[dx]], axis=0), step)

    early = [(1, -1), (3, 1)]
    terms = [both_sent(near_parts, behind_parts, *route) for route in early]
    behind_two = chip_send(behind_parts[2], 2)
    slots = [
        (0, [(near_parts[0], 0), (near_two, 0)] + [(term, 0) for term in terms]),
        (3, [(behind_parts[0], 0), (behind_two, 0)] + [(term, 2 * UNIT) for term in terms]),
    ]
    ahead_parts = share(ahead_sum[0], core_swap(ahead_sum[1]))
    last_parts = share(last_sum[0], core_swap(last_sum[1]))
    terms = [both_sent(ahead_parts, last_parts, *route) for route in ((1, -1), (2, 2), (3, 1))]
    slots += [
        (1, [(ahead_parts[0], 0)] + [(term, 0) for term in terms]),
        (2, [(last_parts[0], 0)] + [(term, 2 * UNIT) for term in terms]),
    ]
    return finish(table, slots)


def solution(mesh):
    placed = (P("row", "col"), P("col", "row"), P("col", "row"), P("row", "col"))
    return jax.shard_map(
        body, mesh=mesh, in_specs=placed, out_specs=P("row", "col"), check_vma=False
    )
```

```python
import jax
import jax.numpy as jnp
from jax import lax
from jax.experimental import pallas as pl
from jax.experimental.pallas import tpu as pltpu
from jax.sharding import PartitionSpec as P

BF16, F32 = jnp.bfloat16, jnp.float32
RING = 4
UNIT = 16
CHUNK = 8 * UNIT
LIMIT = dict(vmem_limit_bytes=14 * 1024 * 1024)
VMEM, ANY = pl.BlockSpec(memory_space=pltpu.VMEM), pl.BlockSpec(memory_space=pl.ANY)
SMEM = pl.BlockSpec(memory_space=pltpu.SMEM)


def chip_send(value, step):
    pairs = [(2 * x + c, 2 * ((x + step) % RING) + c) for x in range(RING) for c in range(2)]
    return lax.ppermute(value, "row", pairs)


def core_swap(value):
    return lax.ppermute(value, "row", [(r, r ^ 1) for r in range(2 * RING)])


def ring_send(value, axis, step):
    pairs = []
    for z in range(RING):
        for y in range(RING):
            to_z, to_y = (z, (y + step) % RING) if axis == "y" else ((z + step) % RING, y)
            pairs.append((RING * z + y, RING * to_z + to_y))
    return lax.ppermute(value, "col", pairs)


def preload(weights, after):
    count, parts = len(weights), 4

    def kernel(*refs):
        sources, outs, sems = refs[:count], refs[-1 - count : -1], refs[-1]
        copies = []
        for m in range(count):
            rows = sources[m].shape[0] // parts
            for n in range(parts):
                block = pl.ds(n * rows, rows)
                copies.append(
                    pltpu.make_async_copy(sources[m].at[block], outs[m].at[block], sems.at[m * parts + n])
                )
        for copy in copies:
            copy.start()
        for copy in copies:
            copy.wait()

    return pl.pallas_call(
        kernel,
        in_specs=[ANY] * (count + len(after)),
        out_specs=[VMEM] * count,
        out_shape=[jax.ShapeDtypeStruct(weight.shape, BF16) for weight in weights],
        scratch_shapes=[pltpu.SemaphoreType.DMA((count * parts,))],
        compiler_params=pltpu.CompilerParams(vmem_limit_bytes=38 * 1024 * 1024),
        cost_estimate=pl.CostEstimate(
            flops=0, bytes_accessed=4 * sum(weight.size for weight in weights), transcendentals=0
        ),
    )(*weights, *after)


def tile_cuts(size):
    step = size // 1024 * 256
    return [(n * step, step) for n in range(3)] + [(3 * step, size - 3 * step)]


def pick(table, tokens, groups):
    depth = tokens.shape[1]

    def kernel(table, tokens, *outs):
        for places, out in zip(groups, outs):
            for n, (chain, k) in enumerate(places):
                start = chain * 64 + lax.rem(table[10 - chain] + k, RING) * UNIT
                out[n] = tokens[pl.ds(pl.multiple_of(start, UNIT), UNIT), :]

    return pl.pallas_call(
        kernel,
        in_specs=[SMEM, VMEM],
        out_specs=[VMEM] * len(groups),
        out_shape=[jax.ShapeDtypeStruct((len(places), UNIT, depth), BF16) for places in groups],
        compiler_params=pltpu.CompilerParams(**LIMIT),
    )(table, tokens)


def behind_of(value, after):
    return pl.pallas_call(
        lambda *refs: None,
        in_specs=[ANY] * (1 + len(after)),
        out_specs=ANY,
        out_shape=jax.ShapeDtypeStruct(value.shape, value.dtype),
        input_output_aliases={0: 0},
        compiler_params=pltpu.CompilerParams(**LIMIT),
    )(value, *after)


def stacked(values, after):
    def kernel(*refs):
        for n in range(len(values)):
            refs[-1][n] = refs[n][...]

    return pl.pallas_call(
        kernel,
        in_specs=[VMEM] * len(values) + [ANY] * len(after),
        out_specs=VMEM,
        out_shape=jax.ShapeDtypeStruct((len(values),) + values[0].shape, BF16),
        compiler_params=pltpu.CompilerParams(**LIMIT),
    )(*values, *after)


def up_gate_kernel(first, layout, count, *refs):
    chunks = len(layout)
    table, gate_w, up_w = refs[:3]
    halves = refs[3:5]
    outs, rows = refs[count:-1], refs[-1]
    width = gate_w.shape[1]
    for n, half in enumerate(halves):
        core = table[8] if n == 0 else 1 - table[8]
        for dx in range(RING):
            for c in range(chunks):
                start = pl.multiple_of(c * CHUNK + 2 * dx * UNIT + core * UNIT, UNIT)
                rows[pl.ds(start, UNIT), :] = half[dx, first + c]
    for kind, weight in enumerate((gate_w, up_w)):
        for start, size in tile_cuts(width):
            value = jnp.dot(
                rows[...], weight[:, start : start + size], preferred_element_type=F32
            ).astype(BF16)
            for c in range(chunks):
                out, block = layout[c][kind]
                outs[out][pl.ds(block * CHUNK, CHUNK), pl.ds(start, size)] = value[
                    c * CHUNK : (c + 1) * CHUNK
                ]


def up_gate(halves, first, layout, table, gate_w, up_w, after=()):
    depth, width = gate_w.shape
    chunks = len(layout)
    places = [place for pair in layout for place in pair]
    outs = 1 + max(place[0] for place in places)
    shape = (CHUNK * (1 + max(place[1] for place in places)), width)
    operands = [table, gate_w, up_w, *halves, *after]
    return pl.pallas_call(
        lambda *refs: up_gate_kernel(first, layout, len(operands), *refs),
        in_specs=[SMEM] + [VMEM] * 4 + [ANY] * len(after),
        out_specs=[VMEM] * outs,
        out_shape=[jax.ShapeDtypeStruct(shape, BF16)] * outs,
        scratch_shapes=[pltpu.VMEM((chunks * CHUNK, depth), BF16)],
        compiler_params=pltpu.CompilerParams(**LIMIT),
        cost_estimate=pl.CostEstimate(
            flops=4 * chunks * CHUNK * depth * width,
            bytes_accessed=4 * depth * width + chunks * CHUNK * (depth + 2 * width) * 2,
            transcendentals=0,
        ),
    )(*operands)


def down_kernel(count, slots, *refs):
    table, weight = refs[:2]
    pieces = refs[2 : 2 + count]
    outs, (rows, stage) = refs[-2 - 2 * slots : -2], refs[-2:]
    core = table[8]
    height = rows.shape[0] // count
    for n, piece in enumerate(pieces):
        rows[pl.ds(n * height, height), :] = piece[...]
    for start, size in tile_cuts(weight.shape[1]):
        part = jnp.dot(rows[...], weight[:, start : start + size], preferred_element_type=F32)
        part = part.astype(BF16).reshape(slots, 2, 2, RING, UNIT, size)
        for s in range(slots):
            for chain in range(2):
                for c in range(2):
                    for dx in range(RING):
                        stage[c, s, dx, chain, :, pl.ds(start, size)] = part[s, chain, c, dx]
    for s in range(slots):
        outs[2 * s][...] = stage[core, s]
        outs[2 * s + 1][...] = stage[1 - core, s]


def down(table, slots, pieces, weight, after=()):
    depth, width = weight.shape
    tokens = 2 * CHUNK * slots
    shape = (RING, 2, UNIT, width)
    operands = [table, weight, *pieces, *after]
    outs = pl.pallas_call(
        lambda *refs: down_kernel(len(pieces), slots, *refs),
        in_specs=[SMEM] + [VMEM] * (1 + len(pieces)) + [ANY] * len(after),
        out_specs=[VMEM] * (2 * slots),
        out_shape=[jax.ShapeDtypeStruct(shape, BF16)] * (2 * slots),
        scratch_shapes=[pltpu.VMEM((tokens, depth), BF16), pltpu.VMEM((2, slots) + shape, BF16)],
        compiler_params=pltpu.CompilerParams(**LIMIT),
        cost_estimate=pl.CostEstimate(
            flops=2 * tokens * depth * width,
            bytes_accessed=2 * (depth * width + tokens * (depth + width)),
            transcendentals=0,
        ),
    )(*operands)
    return [(outs[2 * s], outs[2 * s + 1]) for s in range(slots)]


def place(table, at, pieces):
    def kernel(table, *refs):
        out = refs[-1]
        for k in range(RING):
            start = lax.rem(table[at] + k, RING) * UNIT
            for core in range(2):
                out[pl.ds(pl.multiple_of(start + core * 64, UNIT), UNIT), :] = refs[k][
                    pl.ds(core * UNIT, UNIT), :
                ]

    return pl.pallas_call(
        kernel,
        in_specs=[SMEM] + [VMEM] * RING,
        out_specs=VMEM,
        out_shape=jax.ShapeDtypeStruct((CHUNK, pieces[0].shape[1]), BF16),
        compiler_params=pltpu.CompilerParams(**LIMIT),
    )(table, *pieces)


def half(value, core, after):
    def kernel(value, *refs):
        refs[-1][...] = value[pl.ds(core * 64, 64), :]

    return pl.pallas_call(
        kernel,
        in_specs=[VMEM] + [ANY] * len(after),
        out_specs=VMEM,
        out_shape=jax.ShapeDtypeStruct((64, value.shape[1]), BF16),
        compiler_params=pltpu.CompilerParams(**LIMIT),
    )(value, *after)


def share(mine, theirs):
    def kernel(mine, theirs, *outs):
        for dx, out in enumerate(outs):
            total = mine[dx].astype(F32) + theirs[dx].astype(F32)
            out[...] = total.reshape(out.shape).astype(out.dtype)

    shape = (2 * UNIT, mine.shape[-1])
    return pl.pallas_call(
        kernel,
        in_specs=[VMEM] * 2,
        out_specs=[VMEM] * 4,
        out_shape=[jax.ShapeDtypeStruct(shape, kind) for kind in (F32, BF16, BF16, BF16)],
        compiler_params=pltpu.CompilerParams(**LIMIT),
    )(mine, theirs)


def finish(table, slots):
    arrays = [array for _, terms in slots for array, _ in terms]

    def kernel(table, *refs):
        sources, out = iter(refs[:-1]), refs[-1]
        for k, terms in slots:
            total = None
            for _, first in terms:
                value = next(sources)[pl.ds(first, 2 * UNIT), :].astype(F32)
                total = value if total is None else total + value
            total = total.astype(BF16)
            for chain in range(2):
                start = chain * 64 + lax.rem(table[10 - chain] + k, RING) * UNIT
                out[pl.ds(pl.multiple_of(start, UNIT), UNIT), :] = total[chain * UNIT : (chain + 1) * UNIT]

    return pl.pallas_call(
        kernel,
        in_specs=[SMEM] + [VMEM] * len(arrays),
        out_specs=VMEM,
        out_shape=jax.ShapeDtypeStruct((CHUNK, arrays[0].shape[1]), BF16),
        compiler_params=pltpu.CompilerParams(**LIMIT),
    )(table, *arrays)


def pass_on(both, received):
    def kernel(both, received, out):
        out[:CHUNK, :] = (both[:CHUNK, :].astype(F32) + received[...].astype(F32)).astype(BF16)

    return pl.pallas_call(
        kernel,
        in_specs=[VMEM] * 2,
        out_specs=VMEM,
        out_shape=jax.ShapeDtypeStruct(both.shape, BF16),
        input_output_aliases={0: 0},
        compiler_params=pltpu.CompilerParams(**LIMIT),
    )(both, received)


def blend_kernel(at, outs_parts, act, count, *refs):
    table, arrays, outs = refs[0], refs[1:count], refs[count:]
    height = 2 * UNIT

    def total_of(part):
        total = None
        for array, base, k in part:
            start = base
            if k is not None:
                start = pl.multiple_of(base + lax.rem(table[at] + k, RING) * height, height)
            value = arrays[array][pl.ds(start, height), :].astype(F32)
            total = value if total is None else total + value
        return total

    for parts, out in zip(outs_parts, outs):
        if act:
            gate, up = (total_of(part) for part in parts)
            out[...] = (gate / (1.0 + jnp.exp(-gate)) * up).astype(BF16)
        else:
            for m, part in enumerate(parts):
                out[pl.ds(m * height, height), :] = total_of(part).astype(BF16)


def blend(table, at, arrays, outs_parts, act=False):
    width = arrays[0].shape[1]
    count = 1 + len(arrays)
    heights = [2 * UNIT * (1 if act else len(parts)) for parts in outs_parts]
    return pl.pallas_call(
        lambda *refs: blend_kernel(at, outs_parts, act, count, *refs),
        in_specs=[SMEM] + [VMEM] * len(arrays),
        out_specs=[VMEM] * len(outs_parts),
        out_shape=[jax.ShapeDtypeStruct((height, width), BF16) for height in heights],
        compiler_params=pltpu.CompilerParams(**LIMIT),
    )(table, *arrays)


def body(tokens, gate_w, up_w, down_w):
    col, row = lax.axis_index("col"), lax.axis_index("row")
    z, y, x, core = col // RING, col % RING, row // 2, row % 2
    table = [2 * ((x - b // 2) % RING) + b % 2 for b in range(8)] + [core, z, y]
    table = jnp.stack(table).astype(jnp.int32)

    def other_chips(mine):
        return [mine, chip_send(mine, 1), chip_send(mine, 2), chip_send(mine, -1)]

    groups = (((0, 2), (1, 2)), ((0, 1), (0, 3), (1, 1), (1, 3)), ((0, 0), (1, 0)))
    far_rows, beside_rows, near_rows = pick(table, tokens, groups)
    quarters = other_chips(far_rows)
    gate_w, up_w = preload((gate_w, up_w), after=quarters[:1])
    quarters = stacked(quarters, after=[gate_w])
    rest = other_chips(behind_of(beside_rows, [quarters]))

    far = up_gate(
        (quarters, core_swap(quarters)), 0, [[(0, 0), (1, 0)], [(2, 0), (3, 0)]], table, gate_w, up_w
    )
    rest = stacked(rest, after=far[:1])
    rest = (rest, core_swap(rest))
    routes = [("y", 1), ("y", -1), ("z", 1), ("z", -1)]
    first = [ring_send(value, *route) for value, route in zip(far, routes)]
    beside = up_gate(
        rest, 0, [[(0, 0), (0, 1)], [(1, 1), (1, 0)], [(2, 0), (2, 1)], [(3, 1), (3, 0)]], table, gate_w, up_w
    )
    passed = [pass_on(both, value) for both, value in zip(beside, first)]
    second = [ring_send(value, *route) for value, route in zip(passed, routes)]
    rest = stacked(other_chips(behind_of(near_rows, passed)), after=[])
    rest = (rest, core_swap(rest))
    near = up_gate(rest, 0, [[(0, 0), (1, 0)], [(2, 0), (3, 0)]], table, gate_w, up_w, after=passed)

    hidden = []
    gate = lambda k: [(0, 0, k), (2, 0, k), (3, CHUNK, k)]
    up = lambda k: [(1, 0, k), (3, 0, k), (2, CHUNK, k)]
    for chain, (axis, at) in enumerate((("z", 9), ("y", 10))):
        arrays = [*near[2 * chain : 2 * chain + 2], *second[2 * chain : 2 * chain + 2]]
        ahead, behind = blend(table, at, arrays, [[gate(2), up(1)], [up(2), gate(3)]])
        arrays += [ring_send(ahead, axis, 1), ring_send(behind, axis, -1)]
        more, less = blend(
            table, at, arrays, [[gate(1) + [(4, 0, None)]], [up(3) + [(5, 0, None)]]]
        )
        arrays += [ring_send(more, axis, 1), ring_send(less, axis, -1)]
        block = 2 * UNIT
        terms = [gate(0) + [(5, block, None), (6, 0, None)], up(0) + [(4, block, None), (7, 0, None)]]
        hidden += blend(table, at, arrays, [terms], act=True)

    own = [
        place(table, at, [value, ring_send(value, axis, -1), ring_send(value, axis, 2), ring_send(value, axis, 1)])
        for value, axis, at in zip(hidden, "zy", (9, 10))
    ]

    behind = [ring_send(value, axis, 1) for value, axis in zip(own, "yz")]
    ahead = [ring_send(value, axis, -1) for value, axis in zip(own, "yz")]
    near_sum = down(table, 1, own, down_w)[0]
    near_parts = share(near_sum[0], core_swap(near_sum[1]))
    near_two = chip_send(near_parts[2], 2)
    onward = [(half(b, 0, [near_two]), half(a, 1, [near_two])) for b, a in zip(behind, ahead)]
    distant = []
    for (forward, backward), axis in zip(onward, "yz"):
        distant += [ring_send(forward, axis, 1), ring_send(backward, axis, -1)]
    behind_sum, ahead_sum = (
        down(table, 1, pieces, down_w, after=[*onward[0], *onward[1]])[0] for pieces in (behind, ahead)
    )
    behind_parts = share(behind_sum[0], core_swap(behind_sum[1]))
    last_sum = down(table, 1, distant, down_w, after=behind_parts)[0]

    def both_sent(one, two, dx, step):
        return chip_send(jnp.concatenate([one[dx], two[dx]], axis=0), step)

    early = [(1, -1), (3, 1)]
    terms = [both_sent(near_parts, behind_parts, *route) for route in early]
    behind_two = chip_send(behind_parts[2], 2)
    slots = [
        (0, [(near_parts[0], 0), (near_two, 0)] + [(term, 0) for term in terms]),
        (3, [(behind_parts[0], 0), (behind_two, 0)] + [(term, 2 * UNIT) for term in terms]),
    ]
    ahead_parts = share(ahead_sum[0], core_swap(ahead_sum[1]))
    last_parts = share(last_sum[0], core_swap(last_sum[1]))
    terms = [both_sent(ahead_parts, last_parts, *route) for route in ((1, -1), (2, 2), (3, 1))]
    slots += [
        (1, [(ahead_parts[0], 0)] + [(term, 0) for term in terms]),
        (2, [(last_parts[0], 0)] + [(term, 2 * UNIT) for term in terms]),
    ]
    return finish(table, slots)


def solution(mesh):
    placed = (P("row", "col"), P("col", "row"), P("col", "row"), P("row", "col"))
    return jax.shard_map(
        body, mesh=mesh, in_specs=placed, out_specs=P("row", "col"), check_vma=False
    )
```

```python
import jax
import jax.numpy as jnp
from jax import lax
from jax.experimental import pallas as pl
from jax.experimental.pallas import tpu as pltpu
from jax.sharding import PartitionSpec as P

BF16, F32 = jnp.bfloat16, jnp.float32
RING = 4
UNIT = 16
CHUNK = 8 * UNIT
LIMIT = dict(vmem_limit_bytes=14 * 1024 * 1024)
VMEM, ANY = pl.BlockSpec(memory_space=pltpu.VMEM), pl.BlockSpec(memory_space=pl.ANY)
SMEM = pl.BlockSpec(memory_space=pltpu.SMEM)


def chip_send(value, step):
    pairs = [(2 * x + c, 2 * ((x + step) % RING) + c) for x in range(RING) for c in range(2)]
    return lax.ppermute(value, "row", pairs)


def core_swap(value):
    return lax.ppermute(value, "row", [(r, r ^ 1) for r in range(2 * RING)])


def ring_send(value, axis, step):
    pairs = []
    for z in range(RING):
        for y in range(RING):
            to_z, to_y = (z, (y + step) % RING) if axis == "y" else ((z + step) % RING, y)
            pairs.append((RING * z + y, RING * to_z + to_y))
    return lax.ppermute(value, "col", pairs)


def preload(weights, after):
    count, parts = len(weights), 4

    def kernel(*refs):
        sources, outs, sems = refs[:count], refs[-1 - count : -1], refs[-1]
        copies = []
        for m in range(count):
            rows = sources[m].shape[0] // parts
            for n in range(parts):
                block = pl.ds(n * rows, rows)
                copies.append(
                    pltpu.make_async_copy(sources[m].at[block], outs[m].at[block], sems.at[m * parts + n])
                )
        for copy in copies:
            copy.start()
        for copy in copies:
            copy.wait()

    return pl.pallas_call(
        kernel,
        in_specs=[ANY] * (count + len(after)),
        out_specs=[VMEM] * count,
        out_shape=[jax.ShapeDtypeStruct(weight.shape, BF16) for weight in weights],
        scratch_shapes=[pltpu.SemaphoreType.DMA((count * parts,))],
        compiler_params=pltpu.CompilerParams(vmem_limit_bytes=38 * 1024 * 1024),
        cost_estimate=pl.CostEstimate(
            flops=0, bytes_accessed=4 * sum(weight.size for weight in weights), transcendentals=0
        ),
    )(*weights, *after)


def tile_cuts(size):
    step = size // 1024 * 256
    return [(n * step, step) for n in range(3)] + [(3 * step, size - 3 * step)]


def pick(table, tokens, groups):
    depth = tokens.shape[1]

    def kernel(table, tokens, *outs):
        for places, out in zip(groups, outs):
            for n, (chain, k) in enumerate(places):
                start = chain * 64 + lax.rem(table[10 - chain] + k, RING) * UNIT
                out[n] = tokens[pl.ds(pl.multiple_of(start, UNIT), UNIT), :]

    return pl.pallas_call(
        kernel,
        in_specs=[SMEM, VMEM],
        out_specs=[VMEM] * len(groups),
        out_shape=[jax.ShapeDtypeStruct((len(places), UNIT, depth), BF16) for places in groups],
        compiler_params=pltpu.CompilerParams(**LIMIT),
    )(table, tokens)


def behind_of(value, after):
    return pl.pallas_call(
        lambda *refs: None,
        in_specs=[ANY] * (1 + len(after)),
        out_specs=ANY,
        out_shape=jax.ShapeDtypeStruct(value.shape, value.dtype),
        input_output_aliases={0: 0},
        compiler_params=pltpu.CompilerParams(**LIMIT),
    )(value, *after)


def stacked(values, after):
    def kernel(*refs):
        for n in range(len(values)):
            refs[-1][n] = refs[n][...]

    return pl.pallas_call(
        kernel,
        in_specs=[VMEM] * len(values) + [ANY] * len(after),
        out_specs=VMEM,
        out_shape=jax.ShapeDtypeStruct((len(values),) + values[0].shape, BF16),
        compiler_params=pltpu.CompilerParams(**LIMIT),
    )(*values, *after)


def up_gate_kernel(first, layout, count, *refs):
    chunks = len(layout)
    table, gate_w, up_w = refs[:3]
    halves = refs[3:5]
    outs, rows = refs[count:-1], refs[-1]
    width = gate_w.shape[1]
    for n, half in enumerate(halves):
        core = table[8] if n == 0 else 1 - table[8]
        for dx in range(RING):
            for c in range(chunks):
                start = pl.multiple_of(c * CHUNK + 2 * dx * UNIT + core * UNIT, UNIT)
                rows[pl.ds(start, UNIT), :] = half[dx, first + c]
    for kind, weight in enumerate((gate_w, up_w)):
        for start, size in tile_cuts(width):
            value = jnp.dot(
                rows[...], weight[:, start : start + size], preferred_element_type=F32
            ).astype(BF16)
            for c in range(chunks):
                out, block = layout[c][kind]
                outs[out][pl.ds(block * CHUNK, CHUNK), pl.ds(start, size)] = value[
                    c * CHUNK : (c + 1) * CHUNK
                ]


def up_gate(halves, first, layout, table, gate_w, up_w, after=()):
    depth, width = gate_w.shape
    chunks = len(layout)
    places = [place for pair in layout for place in pair]
    outs = 1 + max(place[0] for place in places)
    shape = (CHUNK * (1 + max(place[1] for place in places)), width)
    operands = [table, gate_w, up_w, *halves, *after]
    return pl.pallas_call(
        lambda *refs: up_gate_kernel(first, layout, len(operands), *refs),
        in_specs=[SMEM] + [VMEM] * 4 + [ANY] * len(after),
        out_specs=[VMEM] * outs,
        out_shape=[jax.ShapeDtypeStruct(shape, BF16)] * outs,
        scratch_shapes=[pltpu.VMEM((chunks * CHUNK, depth), BF16)],
        compiler_params=pltpu.CompilerParams(**LIMIT),
        cost_estimate=pl.CostEstimate(
            flops=4 * chunks * CHUNK * depth * width,
            bytes_accessed=4 * depth * width + chunks * CHUNK * (depth + 2 * width) * 2,
            transcendentals=0,
        ),
    )(*operands)


def down_kernel(count, slots, *refs):
    table, weight = refs[:2]
    pieces = refs[2 : 2 + count]
    outs, (rows, stage) = refs[-2 - 2 * slots : -2], refs[-2:]
    core = table[8]
    height = rows.shape[0] // count
    for n, piece in enumerate(pieces):
        rows[pl.ds(n * height, height), :] = piece[...]
    for start, size in tile_cuts(weight.shape[1]):
        part = jnp.dot(rows[...], weight[:, start : start + size], preferred_element_type=F32)
        part = part.astype(BF16).reshape(slots, 2, 2, RING, UNIT, size)
        for s in range(slots):
            for chain in range(2):
                for c in range(2):
                    for dx in range(RING):
                        stage[c, s, dx, chain, :, pl.ds(start, size)] = part[s, chain, c, dx]
    for s in range(slots):
        outs[2 * s][...] = stage[core, s]
        outs[2 * s + 1][...] = stage[1 - core, s]


def down(table, slots, pieces, weight, after=()):
    depth, width = weight.shape
    tokens = 2 * CHUNK * slots
    shape = (RING, 2, UNIT, width)
    operands = [table, weight, *pieces, *after]
    outs = pl.pallas_call(
        lambda *refs: down_kernel(len(pieces), slots, *refs),
        in_specs=[SMEM] + [VMEM] * (1 + len(pieces)) + [ANY] * len(after),
        out_specs=[VMEM] * (2 * slots),
        out_shape=[jax.ShapeDtypeStruct(shape, BF16)] * (2 * slots),
        scratch_shapes=[pltpu.VMEM((tokens, depth), BF16), pltpu.VMEM((2, slots) + shape, BF16)],
        compiler_params=pltpu.CompilerParams(**LIMIT),
        cost_estimate=pl.CostEstimate(
            flops=2 * tokens * depth * width,
            bytes_accessed=2 * (depth * width + tokens * (depth + width)),
            transcendentals=0,
        ),
    )(*operands)
    return [(outs[2 * s], outs[2 * s + 1]) for s in range(slots)]


def place_kernel(table, *refs):
    pieces, outs = refs[:8], refs[8:]
    for chain in range(2):
        for k in range(RING):
            start = lax.rem(table[9 + chain] + k, RING) * UNIT
            for core in range(2):
                outs[chain][pl.ds(pl.multiple_of(start + core * 64, UNIT), UNIT), :] = pieces[4 * chain + k][
                    pl.ds(core * UNIT, UNIT), :
                ]


def place(table, pieces):
    width = pieces[0].shape[1]
    return pl.pallas_call(
        place_kernel,
        in_specs=[SMEM] + [VMEM] * 8,
        out_specs=[VMEM] * 2,
        out_shape=[jax.ShapeDtypeStruct((CHUNK, width), BF16)] * 2,
        compiler_params=pltpu.CompilerParams(**LIMIT),
    )(table, *pieces)


def half(value, core, after):
    def kernel(value, *refs):
        refs[-1][...] = value[pl.ds(core * 64, 64), :]

    return pl.pallas_call(
        kernel,
        in_specs=[VMEM] + [ANY] * len(after),
        out_specs=VMEM,
        out_shape=jax.ShapeDtypeStruct((64, value.shape[1]), BF16),
        compiler_params=pltpu.CompilerParams(**LIMIT),
    )(value, *after)


def share(mine, theirs):
    def kernel(mine, theirs, *outs):
        for dx, out in enumerate(outs):
            total = mine[dx].astype(F32) + theirs[dx].astype(F32)
            out[...] = total.reshape(out.shape).astype(out.dtype)

    shape = (2 * UNIT, mine.shape[-1])
    return pl.pallas_call(
        kernel,
        in_specs=[VMEM] * 2,
        out_specs=[VMEM] * 4,
        out_shape=[jax.ShapeDtypeStruct(shape, kind) for kind in (F32, BF16, BF16, BF16)],
        compiler_params=pltpu.CompilerParams(**LIMIT),
    )(mine, theirs)


def finish(table, slots):
    arrays = [array for _, terms in slots for array, _ in terms]

    def kernel(table, *refs):
        sources, out = iter(refs[:-1]), refs[-1]
        for k, terms in slots:
            total = None
            for _, first in terms:
                value = next(sources)[pl.ds(first, 2 * UNIT), :].astype(F32)
                total = value if total is None else total + value
            total = total.astype(BF16)
            for chain in range(2):
                start = chain * 64 + lax.rem(table[10 - chain] + k, RING) * UNIT
                out[pl.ds(pl.multiple_of(start, UNIT), UNIT), :] = total[chain * UNIT : (chain + 1) * UNIT]

    return pl.pallas_call(
        kernel,
        in_specs=[SMEM] + [VMEM] * len(arrays),
        out_specs=VMEM,
        out_shape=jax.ShapeDtypeStruct((CHUNK, arrays[0].shape[1]), BF16),
        compiler_params=pltpu.CompilerParams(**LIMIT),
    )(table, *arrays)


def pass_on(both, received):
    def kernel(both, received, out):
        out[:CHUNK, :] = (both[:CHUNK, :].astype(F32) + received[...].astype(F32)).astype(BF16)

    return pl.pallas_call(
        kernel,
        in_specs=[VMEM] * 2,
        out_specs=VMEM,
        out_shape=jax.ShapeDtypeStruct(both.shape, BF16),
        input_output_aliases={0: 0},
        compiler_params=pltpu.CompilerParams(**LIMIT),
    )(both, received)


def blend_kernel(at, outs_parts, act, count, *refs):
    table, arrays, outs = refs[0], refs[1:count], refs[count:]
    height = 2 * UNIT

    def total_of(part):
        total = None
        for array, base, k in part:
            start = base
            if k is not None:
                start = pl.multiple_of(base + lax.rem(table[at] + k, RING) * height, height)
            value = arrays[array][pl.ds(start, height), :].astype(F32)
            total = value if total is None else total + value
        return total

    for parts, out in zip(outs_parts, outs):
        if act:
            gate, up = (total_of(part) for part in parts)
            out[...] = (gate / (1.0 + jnp.exp(-gate)) * up).astype(BF16)
        else:
            for m, part in enumerate(parts):
                out[pl.ds(m * height, height), :] = total_of(part).astype(BF16)


def blend(table, at, arrays, outs_parts, act=False):
    width = arrays[0].shape[1]
    count = 1 + len(arrays)
    heights = [2 * UNIT * (1 if act else len(parts)) for parts in outs_parts]
    return pl.pallas_call(
        lambda *refs: blend_kernel(at, outs_parts, act, count, *refs),
        in_specs=[SMEM] + [VMEM] * len(arrays),
        out_specs=[VMEM] * len(outs_parts),
        out_shape=[jax.ShapeDtypeStruct((height, width), BF16) for height in heights],
        compiler_params=pltpu.CompilerParams(**LIMIT),
    )(table, *arrays)


def body(tokens, gate_w, up_w, down_w):
    col, row = lax.axis_index("col"), lax.axis_index("row")
    z, y, x, core = col // RING, col % RING, row // 2, row % 2
    table = [2 * ((x - b // 2) % RING) + b % 2 for b in range(8)] + [core, z, y]
    table = jnp.stack(table).astype(jnp.int32)

    def other_chips(mine):
        return [mine, chip_send(mine, 1), chip_send(mine, 2), chip_send(mine, -1)]

    groups = (((0, 2), (1, 2)), ((0, 1), (0, 3), (1, 1), (1, 3)), ((0, 0), (1, 0)))
    far_rows, beside_rows, near_rows = pick(table, tokens, groups)
    quarters = other_chips(far_rows)
    gate_w, up_w = preload((gate_w, up_w), after=quarters[:1])
    quarters = stacked(quarters, after=[gate_w])
    rest = other_chips(behind_of(beside_rows, [quarters]))

    far = up_gate(
        (quarters, core_swap(quarters)), 0, [[(0, 0), (1, 0)], [(2, 0), (3, 0)]], table, gate_w, up_w
    )
    rest = stacked(rest, after=far[:1])
    rest = (rest, core_swap(rest))
    routes = [("y", 1), ("y", -1), ("z", 1), ("z", -1)]
    first = [ring_send(value, *route) for value, route in zip(far, routes)]
    beside = up_gate(
        rest, 0, [[(0, 0), (0, 1)], [(1, 1), (1, 0)], [(2, 0), (2, 1)], [(3, 1), (3, 0)]], table, gate_w, up_w
    )
    passed = [pass_on(both, value) for both, value in zip(beside, first)]
    second = [ring_send(value, *route) for value, route in zip(passed, routes)]
    rest = stacked(other_chips(behind_of(near_rows, passed)), after=[])
    rest = (rest, core_swap(rest))
    near = up_gate(rest, 0, [[(0, 0), (1, 0)], [(2, 0), (3, 0)]], table, gate_w, up_w, after=passed)

    hidden = []
    gate = lambda k: [(0, 0, k), (2, 0, k), (3, CHUNK, k)]
    up = lambda k: [(1, 0, k), (3, 0, k), (2, CHUNK, k)]
    for chain, (axis, at) in enumerate((("z", 9), ("y", 10))):
        arrays = [*near[2 * chain : 2 * chain + 2], *second[2 * chain : 2 * chain + 2]]
        ahead, behind = blend(table, at, arrays, [[gate(2), up(1)], [up(2), gate(3)]])
        arrays += [ring_send(ahead, axis, 1), ring_send(behind, axis, -1)]
        more, less = blend(
            table, at, arrays, [[gate(1) + [(4, 0, None)]], [up(3) + [(5, 0, None)]]]
        )
        arrays += [ring_send(more, axis, 1), ring_send(less, axis, -1)]
        block = 2 * UNIT
        terms = [gate(0) + [(5, block, None), (6, 0, None)], up(0) + [(4, block, None), (7, 0, None)]]
        hidden += blend(table, at, arrays, [terms], act=True)

    pieces = []
    for value, axis in zip(hidden, ("z", "y")):
        pieces += [value, ring_send(value, axis, -1), ring_send(value, axis, 2), ring_send(value, axis, 1)]
    own = place(table, pieces)

    behind = [ring_send(value, axis, 1) for value, axis in zip(own, "yz")]
    ahead = [ring_send(value, axis, -1) for value, axis in zip(own, "yz")]
    near_sum = down(table, 1, own, down_w)[0]
    near_parts = share(near_sum[0], core_swap(near_sum[1]))
    near_two = chip_send(near_parts[2], 2)
    onward = [(half(b, 0, [near_two]), half(a, 1, [near_two])) for b, a in zip(behind, ahead)]
    distant = []
    for (forward, backward), axis in zip(onward, "yz"):
        distant += [ring_send(forward, axis, 1), ring_send(backward, axis, -1)]
    behind_sum, ahead_sum = (
        down(table, 1, pieces, down_w, after=[*onward[0], *onward[1]])[0] for pieces in (behind, ahead)
    )
    behind_theirs = core_swap(behind_sum[1])
    behind_parts = share(behind_sum[0], behind_theirs)
    last_sum = down(table, 1, distant, down_w, after=behind_parts)[0]

    ahead_parts = share(ahead_sum[0], core_swap(behind_of(ahead_sum[1], [behind_theirs])))
    last_parts = share(last_sum[0], core_swap(last_sum[1]))

    def sent(parts, dx, step):
        value = jnp.concatenate([part[dx] for part in parts], axis=0) if len(parts) > 1 else parts[0][dx]
        return chip_send(value, step)

    early = [near_parts, behind_parts, ahead_parts]
    ones, threes, twos = sent(early, 1, -1), sent(early, 3, 1), sent(early[1:], 2, 2)
    block = 2 * UNIT
    slots = [
        (0, [(near_parts[0], 0), (near_two, 0), (ones, 0), (threes, 0)]),
        (3, [(behind_parts[0], 0), (twos, 0), (ones, block), (threes, block)]),
        (1, [(ahead_parts[0], 0), (twos, block), (ones, 2 * block), (threes, 2 * block)]),
        (2, [(last_parts[0], 0)] + [(sent([last_parts], *route), 0) for route in ((1, -1), (2, 2), (3, 1))]),
    ]
    return finish(table, slots)


def solution(mesh):
    placed = (P("row", "col"), P("col", "row"), P("col", "row"), P("row", "col"))
    return jax.shard_map(
        body, mesh=mesh, in_specs=placed, out_specs=P("row", "col"), check_vma=False
    )
```

```python
import jax
import jax.numpy as jnp
from jax import lax
from jax.experimental import pallas as pl
from jax.experimental.pallas import tpu as pltpu
from jax.sharding import PartitionSpec as P

BF16, F32 = jnp.bfloat16, jnp.float32
RING = 4
UNIT = 16
CHUNK = 8 * UNIT
LIMIT = dict(vmem_limit_bytes=14 * 1024 * 1024)
VMEM, ANY = pl.BlockSpec(memory_space=pltpu.VMEM), pl.BlockSpec(memory_space=pl.ANY)
SMEM = pl.BlockSpec(memory_space=pltpu.SMEM)


def chip_send(value, step):
    pairs = [(2 * x + c, 2 * ((x + step) % RING) + c) for x in range(RING) for c in range(2)]
    return lax.ppermute(value, "row", pairs)


def core_swap(value):
    return lax.ppermute(value, "row", [(r, r ^ 1) for r in range(2 * RING)])


def ring_send(value, axis, step):
    pairs = []
    for z in range(RING):
        for y in range(RING):
            to_z, to_y = (z, (y + step) % RING) if axis == "y" else ((z + step) % RING, y)
            pairs.append((RING * z + y, RING * to_z + to_y))
    return lax.ppermute(value, "col", pairs)


def preload(weights, after):
    count, parts = len(weights), 4

    def kernel(*refs):
        sources, outs, sems = refs[:count], refs[-1 - count : -1], refs[-1]
        copies = []
        for m in range(count):
            rows = sources[m].shape[0] // parts
            for n in range(parts):
                block = pl.ds(n * rows, rows)
                copies.append(
                    pltpu.make_async_copy(sources[m].at[block], outs[m].at[block], sems.at[m * parts + n])
                )
        for copy in copies:
            copy.start()
        for copy in copies:
            copy.wait()

    return pl.pallas_call(
        kernel,
        in_specs=[ANY] * (count + len(after)),
        out_specs=[VMEM] * count,
        out_shape=[jax.ShapeDtypeStruct(weight.shape, BF16) for weight in weights],
        scratch_shapes=[pltpu.SemaphoreType.DMA((count * parts,))],
        compiler_params=pltpu.CompilerParams(vmem_limit_bytes=38 * 1024 * 1024),
        cost_estimate=pl.CostEstimate(
            flops=0, bytes_accessed=4 * sum(weight.size for weight in weights), transcendentals=0
        ),
    )(*weights, *after)


def tile_cuts(size):
    step = size // 512 * 256
    return [(0, step), (step, size - step)]


def pick(table, tokens, groups):
    depth = tokens.shape[1]

    def kernel(table, tokens, *outs):
        for places, out in zip(groups, outs):
            for n, (chain, k) in enumerate(places):
                start = chain * 64 + lax.rem(table[10 - chain] + k, RING) * UNIT
                out[n] = tokens[pl.ds(pl.multiple_of(start, UNIT), UNIT), :]

    return pl.pallas_call(
        kernel,
        in_specs=[SMEM, VMEM],
        out_specs=[VMEM] * len(groups),
        out_shape=[jax.ShapeDtypeStruct((len(places), UNIT, depth), BF16) for places in groups],
        compiler_params=pltpu.CompilerParams(**LIMIT),
    )(table, tokens)


def behind_of(value, after):
    return pl.pallas_call(
        lambda *refs: None,
        in_specs=[ANY] * (1 + len(after)),
        out_specs=ANY,
        out_shape=jax.ShapeDtypeStruct(value.shape, value.dtype),
        input_output_aliases={0: 0},
        compiler_params=pltpu.CompilerParams(**LIMIT),
    )(value, *after)


def stacked(values, after):
    def kernel(*refs):
        for n in range(len(values)):
            refs[-1][n] = refs[n][...]

    return pl.pallas_call(
        kernel,
        in_specs=[VMEM] * len(values) + [ANY] * len(after),
        out_specs=VMEM,
        out_shape=jax.ShapeDtypeStruct((len(values),) + values[0].shape, BF16),
        compiler_params=pltpu.CompilerParams(**LIMIT),
    )(*values, *after)


def up_gate_kernel(first, layout, count, *refs):
    chunks = len(layout)
    table, gate_w, up_w = refs[:3]
    halves = refs[3:5]
    outs, rows = refs[count:-1], refs[-1]
    width = gate_w.shape[1]
    for n, half in enumerate(halves):
        core = table[8] if n == 0 else 1 - table[8]
        for dx in range(RING):
            for c in range(chunks):
                start = pl.multiple_of(c * CHUNK + 2 * dx * UNIT + core * UNIT, UNIT)
                rows[pl.ds(start, UNIT), :] = half[dx, first + c]
    for kind, weight in enumerate((gate_w, up_w)):
        for start, size in tile_cuts(width):
            value = jnp.dot(
                rows[...], weight[:, start : start + size], preferred_element_type=F32
            ).astype(BF16)
            for c in range(chunks):
                out, block = layout[c][kind]
                outs[out][pl.ds(block * CHUNK, CHUNK), pl.ds(start, size)] = value[
                    c * CHUNK : (c + 1) * CHUNK
                ]


def up_gate(halves, first, layout, table, gate_w, up_w, after=()):
    depth, width = gate_w.shape
    chunks = len(layout)
    places = [place for pair in layout for place in pair]
    outs = 1 + max(place[0] for place in places)
    shape = (CHUNK * (1 + max(place[1] for place in places)), width)
    operands = [table, gate_w, up_w, *halves, *after]
    return pl.pallas_call(
        lambda *refs: up_gate_kernel(first, layout, len(operands), *refs),
        in_specs=[SMEM] + [VMEM] * 4 + [ANY] * len(after),
        out_specs=[VMEM] * outs,
        out_shape=[jax.ShapeDtypeStruct(shape, BF16)] * outs,
        scratch_shapes=[pltpu.VMEM((chunks * CHUNK, depth), BF16)],
        compiler_params=pltpu.CompilerParams(**LIMIT),
        cost_estimate=pl.CostEstimate(
            flops=4 * chunks * CHUNK * depth * width,
            bytes_accessed=4 * depth * width + chunks * CHUNK * (depth + 2 * width) * 2,
            transcendentals=0,
        ),
    )(*operands)


def down_kernel(count, slots, *refs):
    table, weight = refs[:2]
    pieces = refs[2 : 2 + count]
    outs, (rows, stage) = refs[-2 - 2 * slots : -2], refs[-2:]
    core = table[8]
    height = rows.shape[0] // count
    for n, piece in enumerate(pieces):
        rows[pl.ds(n * height, height), :] = piece[...]
    for start, size in tile_cuts(weight.shape[1]):
        part = jnp.dot(rows[...], weight[:, start : start + size], preferred_element_type=F32)
        part = part.astype(BF16).reshape(slots, 2, 2, RING, UNIT, size)
        for s in range(slots):
            for chain in range(2):
                for c in range(2):
                    for dx in range(RING):
                        stage[c, s, dx, chain, :, pl.ds(start, size)] = part[s, chain, c, dx]
    for s in range(slots):
        outs[2 * s][...] = stage[core, s]
        outs[2 * s + 1][...] = stage[1 - core, s]


def down(table, slots, pieces, weight, after=()):
    depth, width = weight.shape
    tokens = 2 * CHUNK * slots
    shape = (RING, 2, UNIT, width)
    operands = [table, weight, *pieces, *after]
    outs = pl.pallas_call(
        lambda *refs: down_kernel(len(pieces), slots, *refs),
        in_specs=[SMEM] + [VMEM] * (1 + len(pieces)) + [ANY] * len(after),
        out_specs=[VMEM] * (2 * slots),
        out_shape=[jax.ShapeDtypeStruct(shape, BF16)] * (2 * slots),
        scratch_shapes=[pltpu.VMEM((tokens, depth), BF16), pltpu.VMEM((2, slots) + shape, BF16)],
        compiler_params=pltpu.CompilerParams(**LIMIT),
        cost_estimate=pl.CostEstimate(
            flops=2 * tokens * depth * width,
            bytes_accessed=2 * (depth * width + tokens * (depth + width)),
            transcendentals=0,
        ),
    )(*operands)
    return [(outs[2 * s], outs[2 * s + 1]) for s in range(slots)]


def place_kernel(table, *refs):
    pieces, outs = refs[:8], refs[8:]
    for chain in range(2):
        for k in range(RING):
            start = lax.rem(table[9 + chain] + k, RING) * UNIT
            for core in range(2):
                outs[chain][pl.ds(pl.multiple_of(start + core * 64, UNIT), UNIT), :] = pieces[4 * chain + k][
                    pl.ds(core * UNIT, UNIT), :
                ]


def place(table, pieces):
    width = pieces[0].shape[1]
    return pl.pallas_call(
        place_kernel,
        in_specs=[SMEM] + [VMEM] * 8,
        out_specs=[VMEM] * 2,
        out_shape=[jax.ShapeDtypeStruct((CHUNK, width), BF16)] * 2,
        compiler_params=pltpu.CompilerParams(**LIMIT),
    )(table, *pieces)


def half(value, core, after):
    def kernel(value, *refs):
        refs[-1][...] = value[pl.ds(core * 64, 64), :]

    return pl.pallas_call(
        kernel,
        in_specs=[VMEM] + [ANY] * len(after),
        out_specs=VMEM,
        out_shape=jax.ShapeDtypeStruct((64, value.shape[1]), BF16),
        compiler_params=pltpu.CompilerParams(**LIMIT),
    )(value, *after)


def share(mine, theirs):
    def kernel(mine, theirs, *outs):
        for dx, out in enumerate(outs):
            total = mine[dx].astype(F32) + theirs[dx].astype(F32)
            out[...] = total.reshape(out.shape).astype(out.dtype)

    shape = (2 * UNIT, mine.shape[-1])
    return pl.pallas_call(
        kernel,
        in_specs=[VMEM] * 2,
        out_specs=[VMEM] * 4,
        out_shape=[jax.ShapeDtypeStruct(shape, kind) for kind in (F32, BF16, BF16, BF16)],
        compiler_params=pltpu.CompilerParams(**LIMIT),
    )(mine, theirs)


def finish(table, slots):
    arrays = [array for _, terms in slots for array, _ in terms]

    def kernel(table, *refs):
        sources, out = iter(refs[:-1]), refs[-1]
        for k, terms in slots:
            total = None
            for _, first in terms:
                value = next(sources)[pl.ds(first, 2 * UNIT), :].astype(F32)
                total = value if total is None else total + value
            total = total.astype(BF16)
            for chain in range(2):
                start = chain * 64 + lax.rem(table[10 - chain] + k, RING) * UNIT
                out[pl.ds(pl.multiple_of(start, UNIT), UNIT), :] = total[chain * UNIT : (chain + 1) * UNIT]

    return pl.pallas_call(
        kernel,
        in_specs=[SMEM] + [VMEM] * len(arrays),
        out_specs=VMEM,
        out_shape=jax.ShapeDtypeStruct((CHUNK, arrays[0].shape[1]), BF16),
        compiler_params=pltpu.CompilerParams(**LIMIT),
    )(table, *arrays)


def pass_on(both, received):
    def kernel(both, received, out):
        out[:CHUNK, :] = (both[:CHUNK, :].astype(F32) + received[...].astype(F32)).astype(BF16)

    return pl.pallas_call(
        kernel,
        in_specs=[VMEM] * 2,
        out_specs=VMEM,
        out_shape=jax.ShapeDtypeStruct(both.shape, BF16),
        input_output_aliases={0: 0},
        compiler_params=pltpu.CompilerParams(**LIMIT),
    )(both, received)


def blend_kernel(at, outs_parts, act, count, *refs):
    table, arrays, outs = refs[0], refs[1:count], refs[count:]
    height = 2 * UNIT

    def total_of(part):
        total = None
        for array, base, k in part:
            start = base
            if k is not None:
                start = pl.multiple_of(base + lax.rem(table[at] + k, RING) * height, height)
            value = arrays[array][pl.ds(start, height), :].astype(F32)
            total = value if total is None else total + value
        return total

    for parts, out in zip(outs_parts, outs):
        if act:
            gate, up = (total_of(part) for part in parts)
            out[...] = (gate / (1.0 + jnp.exp(-gate)) * up).astype(BF16)
        else:
            for m, part in enumerate(parts):
                out[pl.ds(m * height, height), :] = total_of(part).astype(BF16)


def blend(table, at, arrays, outs_parts, act=False):
    width = arrays[0].shape[1]
    count = 1 + len(arrays)
    heights = [2 * UNIT * (1 if act else len(parts)) for parts in outs_parts]
    return pl.pallas_call(
        lambda *refs: blend_kernel(at, outs_parts, act, count, *refs),
        in_specs=[SMEM] + [VMEM] * len(arrays),
        out_specs=[VMEM] * len(outs_parts),
        out_shape=[jax.ShapeDtypeStruct((height, width), BF16) for height in heights],
        compiler_params=pltpu.CompilerParams(**LIMIT),
    )(table, *arrays)


def body(tokens, gate_w, up_w, down_w):
    col, row = lax.axis_index("col"), lax.axis_index("row")
    z, y, x, core = col // RING, col % RING, row // 2, row % 2
    table = [2 * ((x - b // 2) % RING) + b % 2 for b in range(8)] + [core, z, y]
    table = jnp.stack(table).astype(jnp.int32)

    def other_chips(mine):
        return [mine, chip_send(mine, 1), chip_send(mine, 2), chip_send(mine, -1)]

    groups = (((0, 2), (1, 2)), ((0, 1), (0, 3), (1, 1), (1, 3)), ((0, 0), (1, 0)))
    far_rows, beside_rows, near_rows = pick(table, tokens, groups)
    quarters = other_chips(far_rows)
    gate_w, up_w = preload((gate_w, up_w), after=quarters[:1])
    quarters = stacked(quarters, after=[gate_w])
    rest = other_chips(behind_of(beside_rows, [quarters]))

    far = up_gate(
        (quarters, core_swap(quarters)), 0, [[(0, 0), (1, 0)], [(2, 0), (3, 0)]], table, gate_w, up_w
    )
    rest = stacked(rest, after=far[:1])
    rest = (rest, core_swap(rest))
    routes = [("y", 1), ("y", -1), ("z", 1), ("z", -1)]
    first = [ring_send(value, *route) for value, route in zip(far, routes)]
    beside = up_gate(
        rest, 0, [[(0, 0), (0, 1)], [(1, 1), (1, 0)], [(2, 0), (2, 1)], [(3, 1), (3, 0)]], table, gate_w, up_w
    )
    passed = [pass_on(both, value) for both, value in zip(beside, first)]
    second = [ring_send(value, *route) for value, route in zip(passed, routes)]
    rest = stacked(other_chips(behind_of(near_rows, passed)), after=[])
    rest = (rest, core_swap(rest))
    near = up_gate(rest, 0, [[(0, 0), (1, 0)], [(2, 0), (3, 0)]], table, gate_w, up_w, after=passed)

    hidden = []
    gate = lambda k: [(0, 0, k), (2, 0, k), (3, CHUNK, k)]
    up = lambda k: [(1, 0, k), (3, 0, k), (2, CHUNK, k)]
    for chain, (axis, at) in enumerate((("z", 9), ("y", 10))):
        arrays = [*near[2 * chain : 2 * chain + 2], *second[2 * chain : 2 * chain + 2]]
        ahead, behind = blend(table, at, arrays, [[gate(2), up(1)], [up(2), gate(3)]])
        arrays += [ring_send(ahead, axis, 1), ring_send(behind, axis, -1)]
        more, less = blend(
            table, at, arrays, [[gate(1) + [(4, 0, None)]], [up(3) + [(5, 0, None)]]]
        )
        arrays += [ring_send(more, axis, 1), ring_send(less, axis, -1)]
        block = 2 * UNIT
        terms = [gate(0) + [(5, block, None), (6, 0, None)], up(0) + [(4, block, None), (7, 0, None)]]
        hidden += blend(table, at, arrays, [terms], act=True)

    pieces = []
    for value, axis in zip(hidden, ("z", "y")):
        pieces += [value, ring_send(value, axis, -1), ring_send(value, axis, 2), ring_send(value, axis, 1)]
    own = place(table, pieces)

    behind = [ring_send(value, axis, 1) for value, axis in zip(own, "yz")]
    ahead = [ring_send(value, axis, -1) for value, axis in zip(own, "yz")]
    near_sum = down(table, 1, own, down_w)[0]
    near_parts = share(near_sum[0], core_swap(near_sum[1]))
    near_two = chip_send(near_parts[2], 2)
    onward = [(half(b, 0, [near_two]), half(a, 1, [near_two])) for b, a in zip(behind, ahead)]
    distant = []
    for (forward, backward), axis in zip(onward, "yz"):
        distant += [ring_send(forward, axis, 1), ring_send(backward, axis, -1)]
    behind_sum, ahead_sum = (
        down(table, 1, pieces, down_w, after=[*onward[0], *onward[1]])[0] for pieces in (behind, ahead)
    )
    behind_parts = share(behind_sum[0], core_swap(behind_sum[1]))
    last_sum = down(table, 1, distant, down_w, after=behind_parts)[0]

    def both_sent(one, two, dx, step):
        return chip_send(jnp.concatenate([one[dx], two[dx]], axis=0), step)

    early = [(1, -1), (3, 1)]
    terms = [both_sent(near_parts, behind_parts, *route) for route in early]
    behind_two = chip_send(behind_parts[2], 2)
    slots = [
        (0, [(near_parts[0], 0), (near_two, 0)] + [(term, 0) for term in terms]),
        (3, [(behind_parts[0], 0), (behind_two, 0)] + [(term, 2 * UNIT) for term in terms]),
    ]
    ahead_parts = share(ahead_sum[0], core_swap(ahead_sum[1]))
    last_parts = share(last_sum[0], core_swap(last_sum[1]))
    terms = [both_sent(ahead_parts, last_parts, *route) for route in ((1, -1), (2, 2), (3, 1))]
    slots += [
        (1, [(ahead_parts[0], 0)] + [(term, 0) for term in terms]),
        (2, [(last_parts[0], 0)] + [(term, 2 * UNIT) for term in terms]),
    ]
    return finish(table, slots)


def solution(mesh):
    placed = (P("row", "col"), P("col", "row"), P("col", "row"), P("row", "col"))
    return jax.shard_map(
        body, mesh=mesh, in_specs=placed, out_specs=P("row", "col"), check_vma=False
    )
```
